256 devices in a mesh: mem: 128 (over z, y, x), rep: 2 (over core).
Axes of the slice: x: 4, y: 4, z: 8, core: 2. Of those that a mesh axis runs over, the one named last changes fastest.
Arguments:
- particle_vectors: bfloat16 [512, 131072], P('mem', 'rep'), may hold values from -6 to 6
- observed: bfloat16 [512, 131072], P('mem', 'rep'), may hold values from -24 to 24
- precision: float32 [131072], P('rep'), may hold values from 0.5 to 240, as said below
- entry_projection_matrix: bfloat16 [2, 256, 1024], replicated, may hold values from -0.375 to 0.375
- entry_offsets: float32 [2, 1024], replicated, may hold values from -3 to 3
- exit_projection_matrix: bfloat16 [2, 1024, 256], replicated, may hold values from -0.1875 to 0.1875
- exit_offsets: float32 [2, 256], replicated, may hold values from -3 to 3
Outputs:
- updated: bfloat16 [512, 131072], P('mem', 'rep')
The draws below stay inside these ranges and needn't reach their ends.
Inputs may be any that keep to these rules, and one draw needn't show every extreme that they name: `precision`: positive precisions.
All inputs are finite; a program needn't handle non-finite values.
Results may differ from the reference program's by a relative error of at most 0.0065.
Values may be sent and summed in bfloat16 or wider, within the bound.
A program may use at most 64 MiB of HBM per device.

```python
import jax
import jax.numpy as jnp
from jax import lax

PW = 256
HID = 1024
LAYERS = 2
PATCHES = 512
MEMBERS = 512
STATE = 131072
BLOCK = 512


def draw_precision(key, part):
    place = jnp.arange(STATE, dtype=jnp.float32) / STATE
    rising = jnp.exp(jnp.log(3.0) * place)
    rough = jnp.exp(jax.random.uniform(key, (STATE,), jnp.float32, jnp.log(0.5), jnp.log(2.0)))
    block_ids = jnp.arange(STATE, dtype=jnp.int32) // BLOCK
    heavy_blocks = jax.random.randint(jax.random.fold_in(key, 5), (3,), 0, STATE // BLOCK, dtype=jnp.int32)
    is_heavy = jnp.any(block_ids[:, None] == heavy_blocks[None, :], axis=1)
    boost = jnp.where(is_heavy, 40.0, 1.0).astype(jnp.float32)
    return rising * rough * boost


def draw_observed(key, part):
    local_key = jax.random.fold_in(key, 17)
    place = jnp.arange(MEMBERS, dtype=jnp.float32) / max(MEMBERS - 1, 1)
    row_scale = jnp.exp(jnp.log(4.0) * place)
    noise = jnp.clip(jax.random.normal(local_key, (MEMBERS, STATE), jnp.float32), -6.0, 6.0)
    return (noise * row_scale[:, None]).astype(jnp.bfloat16)


def levels(rng, shape, split, low, largest):
    level = 1.0
    for dim, parts in split:
        heights = jax.random.uniform(jax.random.fold_in(jax.random.fold_in(rng, 6), dim), (parts,), jnp.float32, low / len(split), largest / len(split))
        level = level * jnp.repeat(jnp.exp(heights), shape[dim] // parts).reshape((-1,) + (1,) * (len(shape) - 1 - dim))
    return level


def normal_values(own_key, shape, scale, reach, split=(), kind=jnp.bfloat16):
    entries = scale * jax.random.normal(own_key, shape, jnp.float32)
    if split:
        entries = entries * levels(own_key, shape, split, -0.22, 0.18)
    return jnp.clip(entries, -reach, reach).astype(kind)


def setup_inputs(seed: int = 0) -> dict:
    arg_keys = jax.random.split(jax.random.key(seed), 8)
    particle_vectors = normal_values(arg_keys[0], (MEMBERS, STATE), 1.0, 6.0, ((0, 128), (1, 2)))
    observed = draw_observed(jax.random.fold_in(arg_keys[7], 71), 0)
    precision = draw_precision(jax.random.fold_in(arg_keys[7], 71), 0)
    entry_projection_matrix = normal_values(arg_keys[3], (LAYERS, PW, HID), PW ** -0.5, 0.375)
    entry_offsets = normal_values(arg_keys[4], (LAYERS, HID), 0.5, 3.0, (), jnp.float32)
    exit_projection_matrix = normal_values(arg_keys[5], (LAYERS, HID, PW), HID ** -0.5, 0.1875)
    exit_offsets = normal_values(arg_keys[6], (LAYERS, PW), 0.5, 3.0, (), jnp.float32)
    return {"particle_vectors": particle_vectors, "observed": observed, "precision": precision, "entry_projection_matrix": entry_projection_matrix, "entry_offsets": entry_offsets, "exit_projection_matrix": exit_projection_matrix, "exit_offsets": exit_offsets}


def patch_network(particle_index, entry_projection_matrix, entry_offsets, exit_projection_matrix, exit_offsets):
    stream = particle_index.reshape(PATCHES, PW)
    for layer in range(LAYERS):
        pre = jnp.dot(stream.astype(jnp.float32), entry_projection_matrix[layer].astype(jnp.float32), preferred_element_type=jnp.float32) + entry_offsets[layer]
        hidden = jax.nn.silu(pre).astype(jnp.bfloat16)
        stream = (stream.astype(jnp.float32) + jnp.dot(hidden.astype(jnp.float32), exit_projection_matrix[layer].astype(jnp.float32), preferred_element_type=jnp.float32) + exit_offsets[layer]).astype(jnp.bfloat16)
    return stream.reshape(STATE)

def reference(particle_vectors, observed, precision, entry_projection_matrix, entry_offsets, exit_projection_matrix, exit_offsets):
    particle_outcomes = lax.map(lambda particle_index: patch_network(particle_index, entry_projection_matrix, entry_offsets, exit_projection_matrix, exit_offsets), particle_vectors)
    resid = (observed.astype(jnp.float32) - particle_outcomes.astype(jnp.float32)).astype(jnp.bfloat16)
    resid_wide = resid.astype(jnp.float32)
    damping = jnp.sum(resid_wide * resid_wide * precision) / (MEMBERS * STATE) + 1e-06
    pred_wide = particle_outcomes.astype(jnp.float32)
    pred_dev = (pred_wide - jnp.mean(pred_wide, axis=0)).astype(jnp.bfloat16)
    state_wide = particle_vectors.astype(jnp.float32)
    state_dev = (state_wide - jnp.mean(state_wide, axis=0)).astype(jnp.bfloat16)
    weighted = (pred_dev.astype(jnp.float32) * precision).astype(jnp.bfloat16)
    gram = jnp.dot(weighted.astype(jnp.float32), pred_dev.T.astype(jnp.float32), preferred_element_type=jnp.float32) / STATE
    cross = jnp.dot(resid.astype(jnp.float32), weighted.T.astype(jnp.float32), preferred_element_type=jnp.float32) / STATE
    kmat = gram + damping * jnp.eye(MEMBERS, dtype=jnp.float32)
    factor = jnp.linalg.cholesky(kmat)
    middle = jax.scipy.linalg.solve_triangular(factor, cross.T, lower=True)
    solved = jax.scipy.linalg.solve_triangular(factor, middle, lower=True, trans='T')
    mixing = solved.T.astype(jnp.bfloat16)
    return (state_wide + jnp.dot(mixing.astype(jnp.float32), state_dev.astype(jnp.float32), preferred_element_type=jnp.float32)).astype(jnp.bfloat16)
```

```python
import jax
import jax.numpy as jnp
from jax import lax
from jax.experimental import pallas as pl
from jax.experimental.pallas import tpu as pltpu
from jax.sharding import Mesh
from jax.sharding import PartitionSpec as P

PW = 256
LAYERS = 2
MEM = ("mem_0", "mem_1", "mem_2")


def copy_for_each(array, axis):
    copies = jnp.broadcast_to(array, (lax.axis_size(axis), *array.shape))
    return lax.all_to_all(copies, axis, split_axis=0, concat_axis=0, tiled=True)


def over_copies(array, axis):
    return copy_for_each(array, axis).sum(axis=0)


def one_axis_at_a_time(array, axes):
    far, near = axes
    return over_copies(over_copies(array, near), far)


def cut_along(array, dim, length):
    lengths = array.shape
    pieces = array.reshape(*lengths[:dim], length, lengths[dim] // length, *lengths[dim + 1 :])
    return jnp.moveaxis(pieces, dim, 0)


def sent_and_summed(array, axis, dim):
    length = lax.axis_size(axis)
    pieces = lax.all_to_all(cut_along(array, dim, length), axis, 0, 0, tiled=True)
    return jnp.sum(pieces, axis=0)


def sum_by_axis(array, axes, dim):
    far, near = axes
    own = sent_and_summed(cut_along(array, dim, lax.axis_size(far)), near, dim + 1)
    return jnp.sum(lax.all_to_all(own, far, 0, 0, tiled=True), axis=0)


def laid_out(pieces, dim):
    pieces = jnp.moveaxis(pieces, 0, dim)
    lengths = pieces.shape
    return pieces.reshape(*lengths[:dim], lengths[dim] * lengths[dim + 1], *lengths[dim + 2 :])


def whole_of(array, axes, dim):
    far, near = axes
    leading = copy_for_each(array, far)
    pieces = jnp.swapaxes(copy_for_each(leading, near), 0, 1)
    return laid_out(pieces.reshape(-1, *array.shape), dim)


def contract(left, right):
    return lax.dot_general(
        left, right, (((1,), (1,)), ((), ())), preferred_element_type=jnp.float32
    )


F32 = jnp.float32
TILE = 128


def exact_dot(left, right):
    return jnp.dot(left, right, precision=lax.Precision.HIGHEST, preferred_element_type=F32)


def eliminate(a, first):
    sub = lax.broadcasted_iota(jnp.int32, (8, TILE), 0)
    lane = lax.broadcasted_iota(jnp.int32, (8, TILE), 1)
    rows = a[first : first + 8, :]
    own = (lane >= first) & (lane < first + 8)
    fresh = jnp.where(own, jnp.where(lane - first == sub, 1.0, 0.0), rows)
    cols = [jnp.broadcast_to(rows[:, first + j : first + j + 1], (8, TILE)) for j in range(8)]
    for k in range(8):
        inverse = 1.0 / jnp.broadcast_to(cols[k][k : k + 1, :], (8, TILE))
        row = jnp.broadcast_to(fresh[k : k + 1, :], (8, TILE)) * inverse
        fresh = jnp.where(sub == k, row, fresh - cols[k] * row)
        for j in range(k + 1, 8):
            entry = jnp.broadcast_to(cols[j][k : k + 1, :], (8, TILE)) * inverse
            cols[j] = jnp.where(sub == k, entry, cols[j] - cols[k] * entry)
    lanes = lax.broadcasted_iota(jnp.int32, (TILE, TILE), 1)
    rest = jnp.where((lanes >= first) & (lanes < first + 8), 0.0, a)
    for j in range(8):
        left = jnp.broadcast_to(a[:, first + j : first + j + 1], (TILE, TILE))
        rest = rest - left * jnp.broadcast_to(fresh[j : j + 1, :], (TILE, TILE))
    parts = (rest[:first], fresh, rest[first + 8 :])
    return jnp.concatenate([part for part in parts if part.shape[0]], axis=0)


def invert_block(a):
    for first in range(0, TILE, 8):
        a = eliminate(a, first)
    return a


def invert_kernel(k_ref, o_ref):
    o_ref[...] = k_ref[...]

    def step(b, carry):
        own = pl.ds(pl.multiple_of(b * TILE, TILE), TILE)
        block = invert_block(o_ref[own, own])
        rows = exact_dot(block, o_ref[own, :])
        cols = o_ref[:, own]
        o_ref[...] = o_ref[...] - exact_dot(cols, rows)
        o_ref[:, own] = -exact_dot(cols, block)
        o_ref[own, :] = rows
        o_ref[own, own] = block
        return carry

    lax.fori_loop(0, o_ref.shape[0] // TILE, step, 0)


def inverse_of(kmat):
    return pl.pallas_call(
        invert_kernel,
        out_shape=jax.ShapeDtypeStruct(kmat.shape, F32),
        compiler_params=pltpu.CompilerParams(vmem_limit_bytes=32 << 20),
        name="inverse",
    )(kmat)


def body(
    particle_vectors,
    observed,
    precision,
    entry_projection_matrix,
    entry_offsets,
    exit_projection_matrix,
    exit_offsets,
):
    owned, local_width = particle_vectors.shape
    mem_count = lax.axis_size(MEM)
    member_total = owned * mem_count
    state_total = local_width * lax.axis_size("rep")
    axes = (("mem_0", "mem_1"), ("mem_2", "rep"))
    own_states, own_observed = (
        lax.all_to_all(particle_vectors, MEM, split_axis=1, concat_axis=0, tiled=True),
        lax.all_to_all(observed, MEM, split_axis=1, concat_axis=0, tiled=True),
    )
    block_width = own_states.shape[1]
    patches = [own_states[:, at : at + PW] for at in range(0, block_width, PW)]
    stream = jnp.concatenate(patches, axis=0)
    for layer in range(LAYERS):
        pre = (
            jnp.dot(stream, entry_projection_matrix[layer], preferred_element_type=jnp.float32)
            + entry_offsets[layer]
        )
        hidden = jax.nn.silu(pre).astype(jnp.bfloat16)
        stream = (
            stream.astype(jnp.float32)
            + jnp.dot(hidden, exit_projection_matrix[layer], preferred_element_type=jnp.float32)
            + exit_offsets[layer]
        ).astype(jnp.bfloat16)
    own_preds = jnp.concatenate(
        [stream[at : at + member_total] for at in range(0, stream.shape[0], member_total)], axis=1
    )
    prec_block = lax.dynamic_slice_in_dim(precision, lax.axis_index(MEM) * block_width, block_width)
    pred_wide = own_preds.astype(jnp.float32)
    own_resid = (own_observed.astype(jnp.float32) - pred_wide).astype(jnp.bfloat16)
    resid_wide = own_resid.astype(jnp.float32)
    misfit = jnp.sum(resid_wide * resid_wide * prec_block)
    damping = one_axis_at_a_time(misfit, axes) / (member_total * state_total) + 1e-06
    pred_dev = (pred_wide - jnp.mean(pred_wide, axis=0)).astype(jnp.bfloat16)
    state_wide = own_states.astype(jnp.float32)
    state_dev = (state_wide - jnp.mean(state_wide, axis=0)).astype(jnp.bfloat16)
    weighted = (pred_dev.astype(jnp.float32) * prec_block).astype(jnp.bfloat16)
    joint = sum_by_axis(
        jnp.concatenate([contract(weighted, pred_dev), contract(own_resid, weighted)], axis=1),
        axes,
        0,
    )
    gram = whole_of(joint[:, :member_total], axes, 0) / state_total
    cross = joint[:, member_total:] / state_total
    kmat = gram + damping * jnp.eye(member_total, dtype=jnp.float32)
    mixing = exact_dot(cross, inverse_of(kmat)).astype(jnp.bfloat16)
    fresh = (
        state_wide
        + jnp.dot(whole_of(mixing, axes, 0), state_dev, preferred_element_type=jnp.float32)
    ).astype(jnp.bfloat16)
    return lax.all_to_all(fresh, MEM, split_axis=0, concat_axis=1, tiled=True)


def solution(mesh):
    torus = Mesh(
        mesh.devices.reshape(8, 4, 4, mesh.shape["rep"]), ("mem_0", "mem_1", "mem_2", "rep")
    )
    return jax.shard_map(
        body,
        mesh=torus,
        in_specs=(P(MEM, "rep"), P(MEM, "rep"), P("rep"), P(), P(), P(), P()),
        out_specs=P(MEM, "rep"),
        check_vma=False,
    )
```

```python
import functools

import jax
import jax.numpy as jnp
from jax import lax
from jax.experimental import pallas as pl
from jax.experimental.pallas import tpu as pltpu
from jax.sharding import PartitionSpec as P

F32 = jnp.float32
BF16 = jnp.bfloat16
MESH = pl.DeviceIdType.MESH
PW = 256
LAYERS = 2
TILE = 128
NZ, NY, NX = 8, 4, 4
PLANE = NY * NX
PEERS = NZ * PLANE
CORES = 2
MEMBERS = 512
STATE = 131072
OWNED = MEMBERS // PEERS
BLOCK = STATE // CORES // PEERS
TILES = MEMBERS // TILE
LOWER = [(i, j) for i in range(TILES) for j in range(i + 1)]
GRAM_ROWS = len(LOWER) * TILE // CORES // PLANE
CROSS_ROWS = MEMBERS // CORES // PLANE
CHUNK = 256
GROUPS = CHUNK // OWNED


def exact_dot(left, right):
    return jnp.dot(left, right, precision=lax.Precision.HIGHEST, preferred_element_type=F32)


def contract(left, right):
    return lax.dot_general(left, right, (((1,), (1,)), ((), ())), preferred_element_type=F32)


def eliminate(a, first):
    sub = lax.broadcasted_iota(jnp.int32, (8, TILE), 0)
    lane = lax.broadcasted_iota(jnp.int32, (8, TILE), 1)
    rows = a[first : first + 8, :]
    own = (lane >= first) & (lane < first + 8)
    fresh = jnp.where(own, jnp.where(lane - first == sub, 1.0, 0.0), rows)
    cols = [jnp.broadcast_to(rows[:, first + j : first + j + 1], (8, TILE)) for j in range(8)]
    for k in range(8):
        inverse = 1.0 / jnp.broadcast_to(cols[k][k : k + 1, :], (8, TILE))
        row = jnp.broadcast_to(fresh[k : k + 1, :], (8, TILE)) * inverse
        fresh = jnp.where(sub == k, row, fresh - cols[k] * row)
        for j in range(k + 1, 8):
            entry = jnp.broadcast_to(cols[j][k : k + 1, :], (8, TILE)) * inverse
            cols[j] = jnp.where(sub == k, entry, cols[j] - cols[k] * entry)
    lanes = lax.broadcasted_iota(jnp.int32, (TILE, TILE), 1)
    rest = jnp.where((lanes >= first) & (lanes < first + 8), 0.0, a)
    for j in range(8):
        left = jnp.broadcast_to(a[:, first + j : first + j + 1], (TILE, TILE))
        rest = rest - left * jnp.broadcast_to(fresh[j : j + 1, :], (TILE, TILE))
    parts = (rest[:first], fresh, rest[first + 8 :])
    return jnp.concatenate([part for part in parts if part.shape[0]], axis=0)


def invert_block(a):
    for first in range(0, TILE, 8):
        a = eliminate(a, first)
    return a


def invert_step(k_ref, b):
    own = slice(b * TILE, (b + 1) * TILE)
    block = invert_block(k_ref[own, own])
    rows = exact_dot(block, k_ref[own, :])
    cols = k_ref[:, own]
    k_ref[...] = k_ref[...] - exact_dot(cols, rows)
    k_ref[:, own] = -exact_dot(cols, block)
    k_ref[own, :] = rows
    k_ref[own, own] = block


def forecast(x, up_ref, up_bias_ref, down_ref, down_bias_ref):
    for layer in range(LAYERS):
        half = 0.5 * (
            jnp.dot(x, up_ref[layer], preferred_element_type=F32) + up_bias_ref[layer : layer + 1, :]
        )
        hidden = (half + half * jnp.tanh(half)).astype(BF16)
        x = (
            x.astype(F32)
            + jnp.dot(hidden, down_ref[layer], preferred_element_type=F32)
            + down_bias_ref[layer : layer + 1, :]
        ).astype(BF16)
    return x


def wait_for(ref, sem):
    pltpu.make_async_copy(ref, ref, sem).wait()


def kernel(
    x_hbm, obs_hbm, prec_hbm, up_hbm, up_bias, down_hbm, down_bias, out_ref,
    x_own, obs_own, prec_in, prec, up, down, x_in, obs_in, pred, states, dev, weighted, back,
    gram, gram_pair, gram_half, gram_plane, gram_z, gram_all,
    cross, cross_pair, cross_half, cross_plane, cross_z, cross_all, kmat,
    load_sem, own_sem, send_sem, recv_sem,
):
    me, core = lax.axis_index("mem"), lax.axis_index("rep")
    z, q = me // PLANE, lax.rem(me, PLANE)
    y, x = q // NX, lax.rem(q, NX)

    loads = [
        pltpu.make_async_copy(src, dst, load_sem.at[i])
        for i, (src, dst) in enumerate(
            [(up_hbm, up), (down_hbm, down), (prec_hbm, prec_in), (x_hbm, x_own), (obs_hbm, obs_own)]
        )
    ]
    own_copies = [
        pltpu.make_async_copy(x_hbm.at[me], x_in.at[me], own_sem.at[0]),
        pltpu.make_async_copy(obs_hbm.at[me], obs_in.at[me], own_sem.at[1]),
    ]

    def plane_peer(s):
        return lax.rem(y + s // NX, NY) * NX + lax.rem(x + lax.rem(s, NX), NX)

    def peer(s):
        return lax.rem(z + lax.rem(s, NZ), NZ) * PLANE + plane_peer(s // NZ)

    barrier = pltpu.get_barrier_semaphore()

    def greet(s, carry):
        pl.semaphore_signal(barrier, 1, device_id={"mem": peer(s)}, device_id_type=MESH)
        return carry

    pl.semaphore_signal(barrier, 1, device_id={"rep": 1 - core}, device_id_type=MESH)
    lax.fori_loop(1, PEERS, greet, 0)
    for copy in own_copies + loads:
        copy.start()
    pl.semaphore_wait(barrier, PEERS)

    def send(src, dst, i, target):
        pltpu.make_async_remote_copy(
            src_ref=src, dst_ref=dst, send_sem=send_sem.at[i], recv_sem=recv_sem.at[i],
            device_id=target, device_id_type=MESH,
        ).start()

    def exchange(src, dst, i):
        def one(s, carry):
            target = peer(s)
            send(src.at[target], dst.at[me], i, {"mem": target})
            return carry

        lax.fori_loop(1, PEERS, one, 0)

    def to_plane(src_of, dst, i):
        def one(s, carry):
            target = plane_peer(s)
            send(src_of(target), dst, i, {"mem": z * PLANE + target})
            return carry

        lax.fori_loop(1, PLANE, one, 0)

    def to_column(src, dst, i):
        def one(s, carry):
            send(src, dst, i, {"mem": lax.rem(z + s, NZ) * PLANE + q})
            return carry

        lax.fori_loop(1, NZ, one, 0)

    def sum_plane(ref, own_part):
        ref[q] = own_part
        total = ref[0]
        for s in range(1, ref.shape[0]):
            total = total + ref[s]
        return total

    others = pl.ds(0, PEERS - 1)
    exchange(x_hbm, x_in, 0)
    exchange(obs_hbm, obs_in, 1)

    for copy in loads:
        copy.wait()
    for c in range(BLOCK // TILE):
        prec[:, c * TILE : (c + 1) * TILE] = prec_in[pl.ds(c, PEERS, stride=BLOCK // TILE), :]

    def misfit_of(c, total):
        at = pl.ds(pl.multiple_of(c * GROUPS, GROUPS), GROUPS)
        rows = x_own[at].reshape(CHUNK, BLOCK)
        seen = obs_own[at].reshape(CHUNK, BLOCK)
        for p in range(0, BLOCK, PW):
            said = forecast(rows[:, p : p + PW], up, up_bias, down, down_bias)
            resid = (seen[:, p : p + PW].astype(F32) - said.astype(F32)).astype(BF16).astype(F32)
            square = (resid * resid).reshape(GROUPS, OWNED, PW).sum(axis=1)
            total = total + square * prec[at, p : p + PW]
        return total

    misfit = jnp.sum(
        lax.fori_loop(0, MEMBERS // CHUNK, misfit_of, jnp.zeros((GROUPS, PW), F32))
    ) / (MEMBERS * STATE)

    own_copies[0].wait()
    wait_for(x_in.at[others], recv_sem.at[0])

    def forecast_block(c, carry):
        rows = x_in[pl.ds(pl.multiple_of(c * GROUPS, GROUPS), GROUPS)].reshape(CHUNK, BLOCK)
        at = pl.ds(pl.multiple_of(c * CHUNK, CHUNK), CHUNK)
        states[at, :] = rows
        for p in range(0, BLOCK, PW):
            pred[at, p : p + PW] = forecast(rows[:, p : p + PW], up, up_bias, down, down_bias)
        return carry

    lax.fori_loop(0, MEMBERS // CHUNK, forecast_block, 0)
    prec_row = prec[pl.ds(me, 1), :]
    wide = pred[...].astype(F32)
    dev[...] = (wide - jnp.mean(wide, axis=0, keepdims=True)).astype(BF16)
    weighted[...] = (dev[...].astype(F32) * prec_row).astype(BF16)
    eye = lax.broadcasted_iota(jnp.int32, (TILE, TILE), 0) == lax.broadcasted_iota(
        jnp.int32, (TILE, TILE), 1
    )
    for i in range(TILES):
        rows = contract(weighted[i * TILE : (i + 1) * TILE, :], dev[: (i + 1) * TILE, :]) / STATE
        for j in range(i + 1):
            part = rows[:, j * TILE : (j + 1) * TILE]
            if i == j:
                part = part + jnp.where(eye, misfit, 0.0)
            at = LOWER.index((i, j)) * TILE
            gram[at : at + TILE, :] = part

    half = GRAM_ROWS * PLANE
    theirs = pl.ds(pl.multiple_of((1 - core) * half, 8), half)
    send(gram.at[theirs], gram_pair, 2, {"rep": 1 - core})
    wide = states[...].astype(F32)
    dev[...] = (wide - jnp.mean(wide, axis=0, keepdims=True)).astype(BF16)
    wait_for(gram_pair, recv_sem.at[2])
    mine = pl.ds(pl.multiple_of(core * half, 8), half)
    gram_half[...] = (gram[mine, :] + gram_pair[...]).reshape(PLANE, GRAM_ROWS, TILE)
    to_plane(lambda target: gram_half.at[target], gram_plane.at[q], 3)
    wait_for(gram_plane.at[pl.ds(0, PLANE - 1)], recv_sem.at[3])
    gram_z[z] = sum_plane(gram_plane, gram_half[q])
    to_column(gram_z.at[z], gram_z.at[z], 4)
    wait_for(gram_z.at[pl.ds(0, NZ - 1)], recv_sem.at[4])
    total = gram_z[0]
    for s in range(1, NZ):
        total = total + gram_z[s]
    gram_all[core * PLANE + q] = total
    to_plane(lambda target: gram_all.at[core * PLANE + q], gram_all.at[core * PLANE + q], 5)

    own_copies[1].wait()
    wait_for(obs_in.at[others], recv_sem.at[1])
    for c in range(MEMBERS // CHUNK):
        at = slice(c * CHUNK, (c + 1) * CHUNK)
        seen = obs_in[c * GROUPS : (c + 1) * GROUPS].reshape(CHUNK, BLOCK)
        resid = (seen.astype(F32) - pred[at, :].astype(F32)).astype(BF16)
        cross[c] = contract(resid, weighted[...]) / STATE
    send(cross.at[1 - core], cross_pair, 7, {"rep": 1 - core})

    wait_for(gram_all.at[pl.ds(0, PLANE - 1)], recv_sem.at[5])
    summed = pl.ds(pl.multiple_of(core * PLANE, PLANE), PLANE)
    send(gram_all.at[summed], gram_all.at[summed], 6, {"rep": 1 - core})
    wait_for(cross_pair, recv_sem.at[7])
    cross_half[...] = (cross[core] + cross_pair[...]).reshape(PLANE, CROSS_ROWS, MEMBERS)
    to_plane(lambda target: cross_half.at[target], cross_plane.at[q], 8)
    wait_for(gram_all.at[summed], recv_sem.at[6])
    lower = gram_all[...].reshape(len(LOWER) * TILE, TILE)
    below = lax.broadcasted_iota(jnp.int32, (TILE, TILE), 0) >= lax.broadcasted_iota(
        jnp.int32, (TILE, TILE), 1
    )
    for n, (i, j) in enumerate(LOWER):
        part = lower[n * TILE : (n + 1) * TILE, :]
        rows, cols = slice(i * TILE, (i + 1) * TILE), slice(j * TILE, (j + 1) * TILE)
        if i == j:
            kmat[rows, cols] = jnp.where(below, part, part.T) + jnp.where(eye, 1e-06, 0.0)
        else:
            kmat[rows, cols] = part
            kmat[cols, rows] = part.T

    invert_step(kmat, 0)
    wait_for(cross_plane.at[pl.ds(0, PLANE - 1)], recv_sem.at[8])
    cross_z[z] = sum_plane(cross_plane, cross_half[q])
    to_column(cross_z.at[z], cross_z.at[z], 9)
    invert_step(kmat, 1)
    wait_for(cross_z.at[pl.ds(0, NZ - 1)], recv_sem.at[9])
    total = cross_z[0]
    for s in range(1, NZ):
        total = total + cross_z[s]
    cross_all[core * PLANE + q] = total
    to_plane(lambda target: cross_all.at[core * PLANE + q], cross_all.at[core * PLANE + q], 10)
    invert_step(kmat, 2)
    wait_for(cross_all.at[pl.ds(0, PLANE - 1)], recv_sem.at[10])
    send(cross_all.at[summed], cross_all.at[summed], 11, {"rep": 1 - core})
    invert_step(kmat, 3)
    wait_for(cross_all.at[summed], recv_sem.at[11])

    mixing = exact_dot(cross_all[...].reshape(MEMBERS, MEMBERS), kmat[...]).astype(BF16)
    for c in range(MEMBERS // CHUNK):
        at = slice(c * CHUNK, (c + 1) * CHUNK)
        moved = jnp.dot(mixing[at, :], dev[...], preferred_element_type=F32)
        fresh = (states[at, :].astype(F32) + moved).astype(BF16)
        back[c * GROUPS : (c + 1) * GROUPS] = fresh.reshape(GROUPS, OWNED, BLOCK)
    home = pltpu.make_async_copy(back.at[me], out_ref.at[me], own_sem.at[2])
    home.start()
    exchange(back, out_ref, 12)
    home.wait()

    wait_for(x_hbm.at[others], send_sem.at[0])
    wait_for(obs_hbm.at[others], send_sem.at[1])
    wait_for(gram_pair, send_sem.at[2])
    wait_for(gram_plane.at[pl.ds(0, PLANE - 1)], send_sem.at[3])
    wait_for(gram_z.at[pl.ds(0, NZ - 1)], send_sem.at[4])
    wait_for(gram_all.at[pl.ds(0, PLANE - 1)], send_sem.at[5])
    wait_for(gram_all.at[summed], send_sem.at[6])
    wait_for(cross_pair, send_sem.at[7])
    wait_for(cross_plane.at[pl.ds(0, PLANE - 1)], send_sem.at[8])
    wait_for(cross_z.at[pl.ds(0, NZ - 1)], send_sem.at[9])
    wait_for(cross_all.at[pl.ds(0, PLANE - 1)], send_sem.at[10])
    wait_for(cross_all.at[summed], send_sem.at[11])
    wait_for(back.at[others], send_sem.at[12])
    wait_for(out_ref.at[others], recv_sem.at[12])


def body(states, observed, precision, up, up_bias, down, down_bias):
    def by_block(array):
        return array.reshape(OWNED, PEERS, BLOCK).transpose(1, 0, 2)

    anywhere = pl.BlockSpec(memory_space=pl.ANY)
    vmem = pl.BlockSpec(memory_space=pltpu.VMEM)
    slabs = (PEERS, OWNED, BLOCK)
    square = (MEMBERS, BLOCK)
    out = pl.pallas_call(
        kernel,
        out_shape=jax.ShapeDtypeStruct(slabs, BF16),
        in_specs=[anywhere, anywhere, anywhere, anywhere, vmem, anywhere, vmem],
        out_specs=anywhere,
        scratch_shapes=[
            pltpu.VMEM(slabs, BF16),
            pltpu.VMEM(slabs, BF16),
            pltpu.VMEM((PEERS * BLOCK // TILE, TILE), F32),
            pltpu.VMEM((PEERS, BLOCK), F32),
            pltpu.VMEM(up.shape, BF16),
            pltpu.VMEM(down.shape, BF16),
            pltpu.VMEM(slabs, BF16),
            pltpu.VMEM(slabs, BF16),
            pltpu.VMEM(square, BF16),
            pltpu.VMEM(square, BF16),
            pltpu.VMEM(square, BF16),
            pltpu.VMEM(square, BF16),
            pltpu.VMEM(slabs, BF16),
            pltpu.VMEM((len(LOWER) * TILE, TILE), F32),
            pltpu.VMEM((GRAM_ROWS * PLANE, TILE), F32),
            pltpu.VMEM((PLANE, GRAM_ROWS, TILE), F32),
            pltpu.VMEM((PLANE, GRAM_ROWS, TILE), F32),
            pltpu.VMEM((NZ, GRAM_ROWS, TILE), F32),
            pltpu.VMEM((CORES * PLANE, GRAM_ROWS, TILE), F32),
            pltpu.VMEM((CORES, MEMBERS // CORES, MEMBERS), F32),
            pltpu.VMEM((MEMBERS // CORES, MEMBERS), F32),
            pltpu.VMEM((PLANE, CROSS_ROWS, MEMBERS), F32),
            pltpu.VMEM((PLANE, CROSS_ROWS, MEMBERS), F32),
            pltpu.VMEM((NZ, CROSS_ROWS, MEMBERS), F32),
            pltpu.VMEM((CORES * PLANE, CROSS_ROWS, MEMBERS), F32),
            pltpu.VMEM((MEMBERS, MEMBERS), F32),
            pltpu.SemaphoreType.DMA((5,)),
            pltpu.SemaphoreType.DMA((3,)),
            pltpu.SemaphoreType.DMA((13,)),
            pltpu.SemaphoreType.DMA((13,)),
        ],
        compiler_params=pltpu.CompilerParams(
            collective_id=0, has_side_effects=True, vmem_limit_bytes=56 << 20
        ),
        name="ensemble_update",
    )(
        by_block(states),
        by_block(observed),
        precision.reshape(PEERS * BLOCK // TILE, TILE),
        up,
        up_bias,
        down,
        down_bias,
    )
    return out.transpose(1, 0, 2).reshape(OWNED, PEERS * BLOCK)


def solution(mesh):
    return jax.shard_map(
        body,
        mesh=mesh,
        in_specs=(P("mem", "rep"), P("mem", "rep"), P("rep"), P(), P(), P(), P()),
        out_specs=P("mem", "rep"),
        check_vma=False,
    )
```

```python
import functools

import jax
import jax.numpy as jnp
from jax import lax
from jax.experimental import pallas as pl
from jax.experimental.pallas import tpu as pltpu
from jax.sharding import PartitionSpec as P

F32 = jnp.float32
BF16 = jnp.bfloat16
MESH = pl.DeviceIdType.MESH
PW = 256
LAYERS = 2
TILE = 128
NZ, NY, NX = 8, 4, 4
PLANE = NY * NX
PEERS = NZ * PLANE
CORES = 2
MEMBERS = 512
STATE = 131072
OWNED = MEMBERS // PEERS
BLOCK = STATE // CORES // PEERS
TILES = MEMBERS // TILE
LOWER = [(i, j) for i in range(TILES) for j in range(i + 1)]
HEAD = 2
HEAD_ROWS = HEAD * TILE // PLANE
GRAM_ROWS = (len(LOWER) - HEAD) * TILE // CORES // PLANE
PANEL = 16
PARTS = 8
CROSS_ROWS = MEMBERS // CORES // PLANE
CHUNK = 256
GROUPS = CHUNK // OWNED


def exact_dot(left, right):
    return jnp.dot(left, right, precision=lax.Precision.HIGHEST, preferred_element_type=F32)


def contract(left, right):
    return lax.dot_general(left, right, (((1,), (1,)), ((), ())), preferred_element_type=F32)


def repeated(tile, k):
    return jnp.broadcast_to(tile[k : k + 1, :], tile.shape)


def eliminate(a, first):
    tiles = range(PANEL // 8)
    last = first + PANEL
    sub = lax.broadcasted_iota(jnp.int32, (8, TILE), 0)
    lane = lax.broadcasted_iota(jnp.int32, (8, TILE), 1)
    rows = [a[first + 8 * t : first + 8 * t + 8, :] for t in tiles]
    own = (lane >= first) & (lane < last)
    fresh = [jnp.where(own, jnp.where(lane - first == sub + 8 * t, 1.0, 0.0), rows[t]) for t in tiles]
    cols = [
        [jnp.broadcast_to(rows[t][:, first + j : first + j + 1], (8, TILE)) for t in tiles]
        for j in range(PANEL)
    ]
    for k in range(PANEL):
        at, of = divmod(k, 8)
        pivot = cols[k]
        inverse = 1.0 / repeated(pivot[at], of)

        def reduced(column):
            row = repeated(column[at], of) * inverse
            out = [column[t] - pivot[t] * row for t in tiles]
            out[at] = jnp.where(sub == of, row, out[at])
            return out

        for j in range(k + 1, PANEL):
            cols[j] = reduced(cols[j])
        fresh = reduced(fresh)
    block = jnp.concatenate(fresh, axis=0)
    lanes = lax.broadcasted_iota(jnp.int32, (TILE, TILE), 1)
    rest = jnp.where((lanes >= first) & (lanes < last), 0.0, a)
    left = a[:, first:last]
    parts = []
    if first:
        parts.append(rest[:first] - exact_dot(left[:first], block))
    parts.append(block)
    if last < TILE:
        sums = [None] * 4
        for j in range(PANEL):
            term = jnp.broadcast_to(left[last : last + PANEL, j : j + 1], (PANEL, TILE)) * (
                jnp.broadcast_to(block[j : j + 1, :], (PANEL, TILE))
            )
            sums[j % 4] = term if sums[j % 4] is None else sums[j % 4] + term
        parts.append(rest[last : last + PANEL] - ((sums[0] + sums[1]) + (sums[2] + sums[3])))
    if last + PANEL < TILE:
        parts.append(rest[last + PANEL :] - exact_dot(left[last + PANEL :], block))
    return jnp.concatenate(parts, axis=0)


def eliminated(a, begin, end):
    for first in range(begin, end, PANEL):
        a = eliminate(a, first)
    return a


def tile_at(b):
    return slice(b * TILE, (b + 1) * TILE)


def advance(k_ref, b, inverse):
    own, following = tile_at(b), tile_at(b + 1)
    pivot = k_ref[following, following] - exact_dot(
        k_ref[following, own], exact_dot(inverse, k_ref[own, following])
    )
    rows = exact_dot(inverse, k_ref[own, :])
    cols = k_ref[:, own]
    scaled = exact_dot(cols, inverse)
    for i in range(TILES):
        for j in range(TILES):
            at = tile_at(i), tile_at(j)
            if i == b:
                k_ref[at] = inverse if j == b else rows[:, at[1]]
            elif j == b:
                k_ref[at] = -scaled[at[0], :]
            else:
                k_ref[at] = k_ref[at] - exact_dot(cols[at[0], :], rows[:, at[1]])
    return pivot


def forecast(x, up_ref, up_bias_ref, down_ref, down_bias_ref):
    for layer in range(LAYERS):
        half = 0.5 * (
            jnp.dot(x, up_ref[layer], preferred_element_type=F32) + up_bias_ref[layer : layer + 1, :]
        )
        hidden = (half + half * jnp.tanh(half)).astype(BF16)
        x = (
            x.astype(F32)
            + jnp.dot(hidden, down_ref[layer], preferred_element_type=F32)
            + down_bias_ref[layer : layer + 1, :]
        ).astype(BF16)
    return x


def wait_for(ref, sem):
    pltpu.make_async_copy(ref, ref, sem).wait()


def kernel(
    x_hbm, obs_hbm, prec_hbm, up_hbm, up_bias_hbm, down_hbm, down_bias_hbm, out_ref,
    x_own, obs_own, prec_in, prec, up, up_bias, down, down_bias, x_in, obs_in, pred, states, dev, weighted, back,
    head, head_pair, head_half, head_plane, head_z, head_all,
    gram, gram_pair, gram_half, gram_plane, gram_z, gram_all,
    cross, cross_pair, cross_half, cross_plane, cross_z, cross_all, kmat,
    load_sem, own_sem, send_sem, recv_sem,
):
    me, core = lax.axis_index("mem"), lax.axis_index("rep")
    z, q = me // PLANE, lax.rem(me, PLANE)
    y, x = q // NX, lax.rem(q, NX)

    loads = [
        pltpu.make_async_copy(src, dst, load_sem.at[i])
        for i, (src, dst) in enumerate(
            [
                (up_hbm, up), (down_hbm, down), (up_bias_hbm, up_bias), (down_bias_hbm, down_bias),
                (prec_hbm, prec_in), (x_hbm, x_own), (obs_hbm, obs_own),
            ]
        )
    ]
    own_copies = [
        pltpu.make_async_copy(x_hbm.at[me], x_in.at[me], own_sem.at[0]),
        pltpu.make_async_copy(obs_hbm.at[me], obs_in.at[me], own_sem.at[1]),
    ]

    columns = [lax.rem(x + d, NX) for d in range(NX)]
    rows_of = [lax.rem(y + d, NY) * NX for d in range(NY)]
    layers = [lax.rem(z + d, NZ) * PLANE for d in range(NZ)]
    far_first = [4, 5, 3, 6, 2, 7, 1, 0]
    plane_peers = [rows_of[b] + columns[a] for b in (2, 1, 3, 0) for a in (2, 1, 3, 0)][:-1]
    column_peers = [layers[d] + q for d in far_first[:-1]]

    def for_peers(visit):
        def one(s, carry):
            side = lax.rem(y + s // NX + 1, NY) * NX + lax.rem(x + lax.rem(s, NX) + 1, NX)
            for d in far_first:
                visit(layers[d] + side)
            return carry

        lax.fori_loop(0, PLANE - 1, one, 0)
        for target in column_peers:
            visit(target)

    barrier = pltpu.get_barrier_semaphore()

    def greet(target):
        pl.semaphore_signal(barrier, 1, device_id={"mem": target}, device_id_type=MESH)

    for_peers(greet)
    pl.semaphore_signal(barrier, 1, device_id={"rep": 1 - core}, device_id_type=MESH)
    for copy in own_copies + loads:
        copy.start()
    pl.semaphore_wait(barrier, PEERS)

    def send(src, dst, i, target):
        pltpu.make_async_remote_copy(
            src_ref=src, dst_ref=dst, send_sem=send_sem.at[i], recv_sem=recv_sem.at[i],
            device_id=target, device_id_type=MESH,
        ).start()

    def exchange(src, dst, i):
        for_peers(lambda target: send(src.at[target], dst.at[me], i, {"mem": target}))

    def to_plane(src_of, dst, i):
        for target in plane_peers:
            send(src_of(target), dst, i, {"mem": z * PLANE + target})

    def to_column(src, dst, i):
        for target in column_peers:
            send(src, dst, i, {"mem": target})

    def to_core(src, dst, i):
        send(src, dst, i, {"rep": 1 - core})

    def summed(ref):
        total = ref[0]
        for n in range(1, ref.shape[0]):
            total = total + ref[n]
        return total

    def all_but_one(ref):
        return ref.at[pl.ds(0, ref.shape[0] - 1)]

    others = pl.ds(0, PEERS - 1)
    exchange(x_hbm, x_in, 0)
    exchange(obs_hbm, obs_in, 1)

    for copy in loads:
        copy.wait()
    for c in range(BLOCK // TILE):
        prec[:, c * TILE : (c + 1) * TILE] = prec_in[pl.ds(c, PEERS, stride=BLOCK // TILE), :]

    def misfit_of(c, total):
        at = pl.ds(pl.multiple_of(c * GROUPS, GROUPS), GROUPS)
        rows = x_own[at].reshape(CHUNK, BLOCK)
        seen = obs_own[at].reshape(CHUNK, BLOCK)
        for p in range(0, BLOCK, PW):
            said = forecast(rows[:, p : p + PW], up, up_bias, down, down_bias)
            resid = (seen[:, p : p + PW].astype(F32) - said.astype(F32)).astype(BF16).astype(F32)
            square = (resid * resid).reshape(GROUPS, OWNED, PW).sum(axis=1)
            total = total + square * prec[at, p : p + PW]
        return total

    misfit = jnp.sum(
        lax.fori_loop(0, MEMBERS // CHUNK, misfit_of, jnp.zeros((GROUPS, PW), F32))
    ) / (MEMBERS * STATE)

    own_copies[0].wait()
    wait_for(x_in.at[others], recv_sem.at[0])

    def forecast_block(c, carry):
        rows = x_in[pl.ds(pl.multiple_of(c * GROUPS, GROUPS), GROUPS)].reshape(CHUNK, BLOCK)
        at = pl.ds(pl.multiple_of(c * CHUNK, CHUNK), CHUNK)
        states[at, :] = rows
        for p in range(0, BLOCK, PW):
            pred[at, p : p + PW] = forecast(rows[:, p : p + PW], up, up_bias, down, down_bias)
        return carry

    lax.fori_loop(0, MEMBERS // CHUNK, forecast_block, 0)
    prec_row = prec[pl.ds(me, 1), :]
    wide = pred[...].astype(F32)
    dev[...] = (wide - jnp.mean(wide, axis=0, keepdims=True)).astype(BF16)
    weighted[...] = (dev[...].astype(F32) * prec_row).astype(BF16)
    eye = lax.broadcasted_iota(jnp.int32, (TILE, TILE), 0) == lax.broadcasted_iota(
        jnp.int32, (TILE, TILE), 1
    )
    def lower_block(i, j):
        part = contract(weighted[tile_at(i), :], dev[tile_at(j), :]) / STATE
        return part + jnp.where(eye, misfit, 0.0) if i == j else part

    for n, (i, j) in enumerate(LOWER[:HEAD]):
        head[tile_at(n), :] = lower_block(i, j)
    to_core(head, head_pair, 2)
    for n, (i, j) in enumerate(LOWER[HEAD:]):
        gram[tile_at(n), :] = lower_block(i, j)
    half = GRAM_ROWS * PLANE
    theirs = pl.ds(pl.multiple_of((1 - core) * half, 8), half)
    mine = pl.ds(pl.multiple_of(core * half, 8), half)
    to_core(gram.at[theirs], gram_pair, 3)
    wait_for(head_pair, recv_sem.at[2])
    head_half[...] = (head[...] + head_pair[...]).reshape(PLANE, HEAD_ROWS, TILE)
    to_plane(lambda target: head_half.at[target], head_plane.at[q], 4)
    wait_for(gram_pair, recv_sem.at[3])
    gram_half[...] = (gram[mine, :] + gram_pair[...]).reshape(PLANE, GRAM_ROWS, TILE)
    to_plane(lambda target: gram_half.at[target], gram_plane.at[q], 5)

    own_copies[1].wait()
    wait_for(obs_in.at[others], recv_sem.at[1])
    for c in range(MEMBERS // CHUNK):
        at = slice(c * CHUNK, (c + 1) * CHUNK)
        seen = obs_in[c * GROUPS : (c + 1) * GROUPS].reshape(CHUNK, BLOCK)
        resid = (seen.astype(F32) - pred[at, :].astype(F32)).astype(BF16)
        cross[c] = contract(resid, weighted[...]) / STATE
    to_core(cross.at[1 - core], cross_pair, 11)

    wait_for(all_but_one(head_plane), recv_sem.at[4])
    head_plane[q] = head_half[q]
    head_z[z] = summed(head_plane)
    to_column(head_z.at[z], head_z.at[z], 6)
    wait_for(all_but_one(gram_plane), recv_sem.at[5])
    gram_plane[q] = gram_half[q]
    gram_z[z] = summed(gram_plane)
    to_column(gram_z.at[z], gram_z.at[z], 7)
    wait_for(cross_pair, recv_sem.at[11])
    cross_half[...] = (cross[core] + cross_pair[...]).reshape(PLANE, CROSS_ROWS, MEMBERS)
    to_plane(lambda target: cross_half.at[target], cross_plane.at[q], 12)
    wide = states[...].astype(F32)
    dev[...] = (wide - jnp.mean(wide, axis=0, keepdims=True)).astype(BF16)
    wait_for(all_but_one(head_z), recv_sem.at[6])
    head_all[q] = summed(head_z)
    to_plane(lambda target: head_all.at[q], head_all.at[q], 8)
    wait_for(all_but_one(gram_z), recv_sem.at[7])
    own_part = core * PLANE + q
    gram_all[own_part] = summed(gram_z)
    to_plane(lambda target: gram_all.at[own_part], gram_all.at[own_part], 9)
    wait_for(all_but_one(cross_plane), recv_sem.at[12])
    cross_plane[q] = cross_half[q]
    cross_z[z] = summed(cross_plane)
    to_column(cross_z.at[z], cross_z.at[z], 13)

    below = lax.broadcasted_iota(jnp.int32, (TILE, TILE), 0) >= lax.broadcasted_iota(
        jnp.int32, (TILE, TILE), 1
    )

    def place(lower, blocks):
        for n, (i, j) in enumerate(blocks):
            part = lower[tile_at(n), :]
            if i == j:
                part = jnp.where(below, part, part.T) + jnp.where(eye, 1e-06, 0.0)
            else:
                kmat[tile_at(j), tile_at(i)] = part.T
            kmat[tile_at(i), tile_at(j)] = part

    wait_for(all_but_one(head_all), recv_sem.at[8])
    place(head_all[...].reshape(HEAD * TILE, TILE), LOWER[:HEAD])
    inverse = eliminated(kmat[tile_at(0), tile_at(0)], 0, TILE // 2)
    core_part = pl.ds(pl.multiple_of(core * PLANE, PLANE), PLANE)
    wait_for(gram_all.at[pl.ds(0, PLANE - 1)], recv_sem.at[9])
    to_core(gram_all.at[core_part], gram_all.at[core_part], 10)
    inverse = eliminated(inverse, TILE // 2, TILE)
    wait_for(all_but_one(cross_z), recv_sem.at[13])
    cross_all[own_part] = summed(cross_z)
    to_plane(lambda target: cross_all.at[own_part], cross_all.at[own_part], 14)
    wait_for(gram_all.at[core_part], recv_sem.at[10])
    place(gram_all[...].reshape((len(LOWER) - HEAD) * TILE, TILE), LOWER[HEAD:])
    inverse = eliminated(advance(kmat, 0, inverse), 0, TILE)
    wait_for(cross_all.at[pl.ds(0, PLANE - 1)], recv_sem.at[14])
    to_core(cross_all.at[core_part], cross_all.at[core_part], 15)
    inverse = eliminated(advance(kmat, 1, inverse), 0, TILE)
    wait_for(cross_all.at[core_part], recv_sem.at[15])

    pivot = advance(kmat, 2, inverse)
    head_cols = slice(0, MEMBERS - TILE)
    tail_cols = slice(MEMBERS - TILE, MEMBERS)
    whole = cross_all[...].reshape(MEMBERS, MEMBERS)
    before = exact_dot(whole[:, head_cols], kmat[head_cols, head_cols])
    left = whole[:, tail_cols] - exact_dot(whole[:, head_cols], kmat[head_cols, tail_cols])
    inverse = eliminated(pivot, 0, TILE)
    last = exact_dot(left, inverse)
    mixing = jnp.concatenate(
        [before + exact_dot(last, kmat[tail_cols, head_cols]), last], axis=1
    ).astype(BF16)
    for c in range(MEMBERS // CHUNK):
        at = slice(c * CHUNK, (c + 1) * CHUNK)
        moved = jnp.dot(mixing[at, :], dev[...], preferred_element_type=F32)
        fresh = (states[at, :].astype(F32) + moved).astype(BF16)
        back[c * GROUPS : (c + 1) * GROUPS] = fresh.reshape(GROUPS, OWNED, BLOCK)
    home = pltpu.make_async_copy(back.at[me], out_ref.at[me], own_sem.at[2])
    home.start()
    exchange(back, out_ref, 16)
    home.wait()

    wait_for(x_hbm.at[others], send_sem.at[0])
    wait_for(obs_hbm.at[others], send_sem.at[1])
    wait_for(head_pair, send_sem.at[2])
    wait_for(gram_pair, send_sem.at[3])
    wait_for(all_but_one(head_plane), send_sem.at[4])
    wait_for(all_but_one(gram_plane), send_sem.at[5])
    wait_for(all_but_one(head_z), send_sem.at[6])
    wait_for(all_but_one(gram_z), send_sem.at[7])
    wait_for(all_but_one(head_all), send_sem.at[8])
    wait_for(gram_all.at[pl.ds(0, PLANE - 1)], send_sem.at[9])
    wait_for(gram_all.at[core_part], send_sem.at[10])
    wait_for(cross_pair, send_sem.at[11])
    wait_for(all_but_one(cross_plane), send_sem.at[12])
    wait_for(all_but_one(cross_z), send_sem.at[13])
    wait_for(cross_all.at[pl.ds(0, PLANE - 1)], send_sem.at[14])
    wait_for(cross_all.at[core_part], send_sem.at[15])
    wait_for(back.at[others], send_sem.at[16])
    wait_for(out_ref.at[others], recv_sem.at[16])


def copy_kernel(src_ref, dst_ref, sem):
    rows = PEERS // PARTS
    copies = [
        pltpu.make_async_copy(src_ref.at[pl.ds(n * rows, rows)], dst_ref.at[pl.ds(n * rows, rows)], sem.at[n])
        for n in range(PARTS)
    ]
    for copy in copies:
        copy.start()
    for copy in copies:
        copy.wait()


def body(states, observed, precision, up, up_bias, down, down_bias):
    def by_block(array):
        return array.reshape(OWNED, PEERS, BLOCK).transpose(1, 0, 2)

    hbm = pl.BlockSpec(memory_space=pltpu.HBM)
    slabs = (PEERS, OWNED, BLOCK)
    square = (MEMBERS, BLOCK)
    out = pl.pallas_call(
        kernel,
        out_shape=jax.ShapeDtypeStruct(slabs, BF16),
        in_specs=[hbm] * 7,
        out_specs=pl.BlockSpec(memory_space=pl.ANY),
        scratch_shapes=[
            pltpu.VMEM(slabs, BF16),
            pltpu.VMEM(slabs, BF16),
            pltpu.VMEM((PEERS * BLOCK // TILE, TILE), F32),
            pltpu.VMEM((PEERS, BLOCK), F32),
            pltpu.VMEM(up.shape, BF16),
            pltpu.VMEM(up_bias.shape, F32),
            pltpu.VMEM(down.shape, BF16),
            pltpu.VMEM(down_bias.shape, F32),
            pltpu.VMEM(slabs, BF16),
            pltpu.VMEM(slabs, BF16),
            pltpu.VMEM(square, BF16),
            pltpu.VMEM(square, BF16),
            pltpu.VMEM(square, BF16),
            pltpu.VMEM(square, BF16),
            pltpu.VMEM(slabs, BF16),
            pltpu.VMEM((HEAD * TILE, TILE), F32),
            pltpu.VMEM((HEAD * TILE, TILE), F32),
            pltpu.VMEM((PLANE, HEAD_ROWS, TILE), F32),
            pltpu.VMEM((PLANE, HEAD_ROWS, TILE), F32),
            pltpu.VMEM((NZ, HEAD_ROWS, TILE), F32),
            pltpu.VMEM((PLANE, HEAD_ROWS, TILE), F32),
            pltpu.VMEM(((len(LOWER) - HEAD) * TILE, TILE), F32),
            pltpu.VMEM((GRAM_ROWS * PLANE, TILE), F32),
            pltpu.VMEM((PLANE, GRAM_ROWS, TILE), F32),
            pltpu.VMEM((PLANE, GRAM_ROWS, TILE), F32),
            pltpu.VMEM((NZ, GRAM_ROWS, TILE), F32),
            pltpu.VMEM((CORES * PLANE, GRAM_ROWS, TILE), F32),
            pltpu.VMEM((CORES, MEMBERS // CORES, MEMBERS), F32),
            pltpu.VMEM((MEMBERS // CORES, MEMBERS), F32),
            pltpu.VMEM((PLANE, CROSS_ROWS, MEMBERS), F32),
            pltpu.VMEM((PLANE, CROSS_ROWS, MEMBERS), F32),
            pltpu.VMEM((NZ, CROSS_ROWS, MEMBERS), F32),
            pltpu.VMEM((CORES * PLANE, CROSS_ROWS, MEMBERS), F32),
            pltpu.VMEM((MEMBERS, MEMBERS), F32),
            pltpu.SemaphoreType.DMA((7,)),
            pltpu.SemaphoreType.DMA((3,)),
            pltpu.SemaphoreType.DMA((17,)),
            pltpu.SemaphoreType.DMA((17,)),
        ],
        compiler_params=pltpu.CompilerParams(
            collective_id=0, has_side_effects=True, vmem_limit_bytes=56 << 20
        ),
        name="ensemble_update",
    )(
        by_block(states),
        by_block(observed),
        precision.reshape(PEERS * BLOCK // TILE, TILE),
        up,
        up_bias,
        down,
        down_bias,
    )
    out = pl.pallas_call(
        copy_kernel,
        out_shape=jax.ShapeDtypeStruct(slabs, BF16),
        in_specs=[hbm],
        out_specs=hbm,
        scratch_shapes=[pltpu.SemaphoreType.DMA((PARTS,))],
        name="copy_out",
    )(out)
    return out.transpose(1, 0, 2).reshape(OWNED, PEERS * BLOCK)


def solution(mesh):
    return jax.shard_map(
        body,
        mesh=mesh,
        in_specs=(P("mem", "rep"), P("mem", "rep"), P("rep"), P(), P(), P(), P()),
        out_specs=P("mem", "rep"),
        check_vma=False,
    )
```

```python
import functools

import jax
import jax.numpy as jnp
from jax import lax
from jax.experimental import pallas as pl
from jax.experimental.pallas import tpu as pltpu
from jax.sharding import PartitionSpec as P

F32 = jnp.float32
BF16 = jnp.bfloat16
MESH = pl.DeviceIdType.MESH
PW = 256
LAYERS = 2
TILE = 128
NZ, NY, NX = 8, 4, 4
PLANE = NY * NX
PEERS = NZ * PLANE
CORES = 2
MEMBERS = 512
STATE = 131072
OWNED = MEMBERS // PEERS
BLOCK = STATE // CORES // PEERS
TILES = MEMBERS // TILE
LOWER = [(i, j) for i in range(TILES) for j in range(i + 1)]
HEAD = 2
HEAD_ROWS = HEAD * TILE // PLANE
GRAM_ROWS = (len(LOWER) - HEAD) * TILE // CORES // PLANE
PANEL = 16
CROSS_ROWS = MEMBERS // CORES // PLANE
CHUNK = 256
GROUPS = CHUNK // OWNED


def exact_dot(left, right):
    return jnp.dot(left, right, precision=lax.Precision.HIGHEST, preferred_element_type=F32)


def contract(left, right):
    return lax.dot_general(left, right, (((1,), (1,)), ((), ())), preferred_element_type=F32)


def repeated(tile, k):
    return jnp.broadcast_to(tile[k : k + 1, :], tile.shape)


def eliminate(a, first):
    tiles = range(PANEL // 8)
    last = first + PANEL
    sub = lax.broadcasted_iota(jnp.int32, (8, TILE), 0)
    lane = lax.broadcasted_iota(jnp.int32, (8, TILE), 1)
    rows = [a[first + 8 * t : first + 8 * t + 8, :] for t in tiles]
    own = (lane >= first) & (lane < last)
    fresh = [jnp.where(own, jnp.where(lane - first == sub + 8 * t, 1.0, 0.0), rows[t]) for t in tiles]
    cols = [
        [jnp.broadcast_to(rows[t][:, first + j : first + j + 1], (8, TILE)) for t in tiles]
        for j in range(PANEL)
    ]
    for k in range(PANEL):
        at, of = divmod(k, 8)
        pivot = cols[k]
        inverse = 1.0 / repeated(pivot[at], of)

        def reduced(column):
            row = repeated(column[at], of) * inverse
            out = [column[t] - pivot[t] * row for t in tiles]
            out[at] = jnp.where(sub == of, row, out[at])
            return out

        for j in range(k + 1, PANEL):
            cols[j] = reduced(cols[j])
        fresh = reduced(fresh)
    block = jnp.concatenate(fresh, axis=0)
    lanes = lax.broadcasted_iota(jnp.int32, (TILE, TILE), 1)
    rest = jnp.where((lanes >= first) & (lanes < last), 0.0, a)
    left = a[:, first:last]
    parts = []
    if first:
        parts.append(rest[:first] - exact_dot(left[:first], block))
    parts.append(block)
    if last < TILE:
        sums = [None] * 4
        for j in range(PANEL):
            term = jnp.broadcast_to(left[last : last + PANEL, j : j + 1], (PANEL, TILE)) * (
                jnp.broadcast_to(block[j : j + 1, :], (PANEL, TILE))
            )
            sums[j % 4] = term if sums[j % 4] is None else sums[j % 4] + term
        parts.append(rest[last : last + PANEL] - ((sums[0] + sums[1]) + (sums[2] + sums[3])))
    if last + PANEL < TILE:
        parts.append(rest[last + PANEL :] - exact_dot(left[last + PANEL :], block))
    return jnp.concatenate(parts, axis=0)


def eliminated(a, begin, end):
    for first in range(begin, end, PANEL):
        a = eliminate(a, first)
    return a


def tile_at(b):
    return slice(b * TILE, (b + 1) * TILE)


def advance(k_ref, b, inverse):
    own, following = tile_at(b), tile_at(b + 1)
    pivot = k_ref[following, following] - exact_dot(
        k_ref[following, own], exact_dot(inverse, k_ref[own, following])
    )
    rows = exact_dot(inverse, k_ref[own, :])
    cols = k_ref[:, own]
    scaled = exact_dot(cols, inverse)
    for i in range(TILES):
        for j in range(TILES):
            at = tile_at(i), tile_at(j)
            if i == b:
                k_ref[at] = inverse if j == b else rows[:, at[1]]
            elif j == b:
                k_ref[at] = -scaled[at[0], :]
            else:
                k_ref[at] = k_ref[at] - exact_dot(cols[at[0], :], rows[:, at[1]])
    return pivot


def forecast(x, up_ref, up_bias_ref, down_ref, down_bias_ref):
    for layer in range(LAYERS):
        half = 0.5 * (
            jnp.dot(x, up_ref[layer], preferred_element_type=F32) + up_bias_ref[layer : layer + 1, :]
        )
        hidden = (half + half * jnp.tanh(half)).astype(BF16)
        x = (
            x.astype(F32)
            + jnp.dot(hidden, down_ref[layer], preferred_element_type=F32)
            + down_bias_ref[layer : layer + 1, :]
        ).astype(BF16)
    return x


def wait_for(ref, sem):
    pltpu.make_async_copy(ref, ref, sem).wait()


def kernel(
    x_hbm, obs_hbm, prec_hbm, up_hbm, up_bias_hbm, down_hbm, down_bias_hbm, out_ref,
    x_own, obs_own, prec_in, prec, up, up_bias, down, down_bias, x_in, obs_in, pred, states, dev, weighted, back,
    head, head_pair, head_half, head_plane, head_z, head_all,
    gram, gram_pair, gram_half, gram_plane, gram_z, gram_all,
    cross, cross_pair, cross_half, cross_plane, cross_z, cross_all, kmat,
    load_sem, own_sem, send_sem, recv_sem, plane_in,
):
    me, core = lax.axis_index("mem"), lax.axis_index("rep")
    z, q = me // PLANE, lax.rem(me, PLANE)
    y, x = q // NX, lax.rem(q, NX)

    loads = [
        pltpu.make_async_copy(src, dst, load_sem.at[i])
        for i, (src, dst) in enumerate(
            [
                (up_hbm, up), (down_hbm, down), (up_bias_hbm, up_bias), (down_bias_hbm, down_bias),
                (prec_hbm, prec_in), (x_hbm, x_own), (obs_hbm, obs_own),
            ]
        )
    ]
    own_copies = [
        pltpu.make_async_copy(x_hbm.at[me], x_in.at[me], own_sem.at[0]),
        pltpu.make_async_copy(obs_hbm.at[me], obs_in.at[me], own_sem.at[1]),
    ]

    columns = [lax.rem(x + d, NX) for d in range(NX)]
    rows_of = [lax.rem(y + d, NY) * NX for d in range(NY)]
    layers = [lax.rem(z + d, NZ) * PLANE for d in range(NZ)]
    far_first = [4, 5, 3, 6, 2, 7, 1, 0]
    plane_peers = [rows_of[b] + columns[a] for b in (2, 1, 3, 0) for a in (2, 1, 3, 0)][:-1]
    column_peers = [layers[d] + q for d in far_first[:-1]]

    def for_peers(visit):
        def one(s, carry):
            side = lax.rem(y + s // NX + 1, NY) * NX + lax.rem(x + lax.rem(s, NX) + 1, NX)
            for d in far_first:
                visit(layers[d] + side)
            return carry

        lax.fori_loop(0, PLANE - 1, one, 0)
        for target in column_peers:
            visit(target)

    barrier = pltpu.get_barrier_semaphore()

    def greet(sem, targets):
        for target in targets:
            pl.semaphore_signal(sem, 1, device_id={"mem": target}, device_id_type=MESH)

    near = [z * PLANE + target for target in plane_peers]
    greet(barrier, near + column_peers)
    pl.semaphore_signal(barrier, 1, device_id={"rep": 1 - core}, device_id_type=MESH)
    for copy in own_copies + loads:
        copy.start()
    pl.semaphore_wait(barrier, PLANE + NZ - 1)
    greet(plane_in, column_peers)
    pl.semaphore_wait(plane_in, NZ - 1)

    def send(src, dst, i, target):
        pltpu.make_async_remote_copy(
            src_ref=src, dst_ref=dst, send_sem=send_sem.at[i], recv_sem=recv_sem.at[i],
            device_id=target, device_id_type=MESH,
        ).start()

    def exchange(src, dst, i):
        for_peers(lambda target: send(src.at[target], dst.at[me], i, {"mem": target}))

    def to_plane(src_of, dst, i):
        for target in plane_peers:
            send(src_of(target), dst, i, {"mem": z * PLANE + target})

    def to_column(src, dst, i):
        for target in column_peers:
            send(src, dst, i, {"mem": target})

    def to_core(src, dst, i):
        send(src, dst, i, {"rep": 1 - core})

    def summed(ref):
        total = ref[0]
        for n in range(1, ref.shape[0]):
            total = total + ref[n]
        return total

    def all_but_one(ref):
        return ref.at[pl.ds(0, ref.shape[0] - 1)]

    others = pl.ds(0, PEERS - 1)
    exchange(x_hbm, x_in, 0)
    exchange(obs_hbm, obs_in, 1)

    for copy in loads:
        copy.wait()
    for c in range(BLOCK // TILE):
        prec[:, c * TILE : (c + 1) * TILE] = prec_in[pl.ds(c, PEERS, stride=BLOCK // TILE), :]

    def misfit_of(c, total):
        at = pl.ds(pl.multiple_of(c * GROUPS, GROUPS), GROUPS)
        rows = x_own[at].reshape(CHUNK, BLOCK)
        seen = obs_own[at].reshape(CHUNK, BLOCK)
        for p in range(0, BLOCK, PW):
            said = forecast(rows[:, p : p + PW], up, up_bias, down, down_bias)
            resid = (seen[:, p : p + PW].astype(F32) - said.astype(F32)).astype(BF16).astype(F32)
            square = (resid * resid).reshape(GROUPS, OWNED, PW).sum(axis=1)
            total = total + square * prec[at, p : p + PW]
        return total

    misfit = jnp.sum(
        lax.fori_loop(0, MEMBERS // CHUNK, misfit_of, jnp.zeros((GROUPS, PW), F32))
    ) / (MEMBERS * STATE)

    own_copies[0].wait()
    wait_for(x_in.at[others], recv_sem.at[0])

    def forecast_block(c, carry):
        rows = x_in[pl.ds(pl.multiple_of(c * GROUPS, GROUPS), GROUPS)].reshape(CHUNK, BLOCK)
        at = pl.ds(pl.multiple_of(c * CHUNK, CHUNK), CHUNK)
        states[at, :] = rows
        for p in range(0, BLOCK, PW):
            pred[at, p : p + PW] = forecast(rows[:, p : p + PW], up, up_bias, down, down_bias)
        return carry

    lax.fori_loop(0, MEMBERS // CHUNK, forecast_block, 0)
    prec_row = prec[pl.ds(me, 1), :]
    wide = pred[...].astype(F32)
    dev[...] = (wide - jnp.mean(wide, axis=0, keepdims=True)).astype(BF16)
    weighted[...] = (dev[...].astype(F32) * prec_row).astype(BF16)
    eye = lax.broadcasted_iota(jnp.int32, (TILE, TILE), 0) == lax.broadcasted_iota(
        jnp.int32, (TILE, TILE), 1
    )
    def lower_block(i, j):
        part = contract(weighted[tile_at(i), :], dev[tile_at(j), :]) / STATE
        return part + jnp.where(eye, misfit, 0.0) if i == j else part

    for n, (i, j) in enumerate(LOWER[:HEAD]):
        head[tile_at(n), :] = lower_block(i, j)
    to_core(head, head_pair, 2)
    for n, (i, j) in enumerate(LOWER[HEAD:]):
        gram[tile_at(n), :] = lower_block(i, j)
    half = GRAM_ROWS * PLANE
    theirs = pl.ds(pl.multiple_of((1 - core) * half, 8), half)
    mine = pl.ds(pl.multiple_of(core * half, 8), half)
    to_core(gram.at[theirs], gram_pair, 3)
    wait_for(head_pair, recv_sem.at[2])
    head_half[...] = (head[...] + head_pair[...]).reshape(PLANE, HEAD_ROWS, TILE)
    to_plane(lambda target: head_half.at[target], head_plane.at[q], 4)
    wait_for(gram_pair, recv_sem.at[3])
    gram_half[...] = (gram[mine, :] + gram_pair[...]).reshape(PLANE, GRAM_ROWS, TILE)
    to_plane(lambda target: gram_half.at[target], gram_plane.at[q], 5)

    own_copies[1].wait()
    wait_for(obs_in.at[others], recv_sem.at[1])
    for c in range(MEMBERS // CHUNK):
        at = slice(c * CHUNK, (c + 1) * CHUNK)
        seen = obs_in[c * GROUPS : (c + 1) * GROUPS].reshape(CHUNK, BLOCK)
        resid = (seen.astype(F32) - pred[at, :].astype(F32)).astype(BF16)
        cross[c] = contract(resid, weighted[...]) / STATE
    to_core(cross.at[1 - core], cross_pair, 11)

    wait_for(all_but_one(head_plane), recv_sem.at[4])
    head_plane[q] = head_half[q]
    head_z[z] = summed(head_plane)
    to_column(head_z.at[z], head_z.at[z], 6)
    wait_for(all_but_one(gram_plane), recv_sem.at[5])
    gram_plane[q] = gram_half[q]
    gram_z[z] = summed(gram_plane)
    to_column(gram_z.at[z], gram_z.at[z], 7)
    wait_for(cross_pair, recv_sem.at[11])
    cross_half[...] = (cross[core] + cross_pair[...]).reshape(PLANE, CROSS_ROWS, MEMBERS)
    to_plane(lambda target: cross_half.at[target], cross_plane.at[q], 12)
    wide = states[...].astype(F32)
    dev[...] = (wide - jnp.mean(wide, axis=0, keepdims=True)).astype(BF16)
    wait_for(all_but_one(head_z), recv_sem.at[6])
    head_all[q] = summed(head_z)
    to_plane(lambda target: head_all.at[q], head_all.at[q], 8)
    wait_for(all_but_one(gram_z), recv_sem.at[7])
    own_part = core * PLANE + q
    gram_all[own_part] = summed(gram_z)
    to_plane(lambda target: gram_all.at[own_part], gram_all.at[own_part], 9)
    wait_for(all_but_one(cross_plane), recv_sem.at[12])
    cross_plane[q] = cross_half[q]
    cross_z[z] = summed(cross_plane)
    to_column(cross_z.at[z], cross_z.at[z], 13)

    below = lax.broadcasted_iota(jnp.int32, (TILE, TILE), 0) >= lax.broadcasted_iota(
        jnp.int32, (TILE, TILE), 1
    )

    def place(lower, blocks):
        for n, (i, j) in enumerate(blocks):
            part = lower[tile_at(n), :]
            if i == j:
                part = jnp.where(below, part, part.T) + jnp.where(eye, 1e-06, 0.0)
            else:
                kmat[tile_at(j), tile_at(i)] = part.T
            kmat[tile_at(i), tile_at(j)] = part

    wait_for(all_but_one(head_all), recv_sem.at[8])
    place(head_all[...].reshape(HEAD * TILE, TILE), LOWER[:HEAD])
    inverse = eliminated(kmat[tile_at(0), tile_at(0)], 0, TILE // 2)
    core_part = pl.ds(pl.multiple_of(core * PLANE, PLANE), PLANE)
    wait_for(gram_all.at[pl.ds(0, PLANE - 1)], recv_sem.at[9])
    to_core(gram_all.at[core_part], gram_all.at[core_part], 10)
    inverse = eliminated(inverse, TILE // 2, TILE)
    wait_for(all_but_one(cross_z), recv_sem.at[13])
    cross_all[own_part] = summed(cross_z)
    to_plane(lambda target: cross_all.at[own_part], cross_all.at[own_part], 14)
    wait_for(gram_all.at[core_part], recv_sem.at[10])
    place(gram_all[...].reshape((len(LOWER) - HEAD) * TILE, TILE), LOWER[HEAD:])
    inverse = eliminated(advance(kmat, 0, inverse), 0, TILE)
    inverse = eliminated(advance(kmat, 1, inverse), 0, TILE)
    wait_for(cross_all.at[pl.ds(0, PLANE - 1)], recv_sem.at[14])
    to_core(cross_all.at[core_part], cross_all.at[core_part], 15)
    inverse = eliminated(advance(kmat, 2, inverse), 0, TILE // 2)
    wait_for(cross_all.at[core_part], recv_sem.at[15])

    head_cols = slice(0, MEMBERS - TILE)
    tail_cols = slice(MEMBERS - TILE, MEMBERS)
    whole = cross_all[...].reshape(MEMBERS, MEMBERS)
    before = exact_dot(whole[:, head_cols], kmat[head_cols, head_cols])
    left = whole[:, tail_cols] - exact_dot(whole[:, head_cols], kmat[head_cols, tail_cols])
    inverse = eliminated(inverse, TILE // 2, TILE)
    last = exact_dot(left, inverse)
    mixing = jnp.concatenate(
        [before + exact_dot(last, kmat[tail_cols, head_cols]), last], axis=1
    ).astype(BF16)
    for c in range(MEMBERS // CHUNK):
        at = slice(c * CHUNK, (c + 1) * CHUNK)
        moved = jnp.dot(mixing[at, :], dev[...], preferred_element_type=F32)
        fresh = (states[at, :].astype(F32) + moved).astype(BF16)
        back[c * GROUPS : (c + 1) * GROUPS] = fresh.reshape(GROUPS, OWNED, BLOCK)
    home = pltpu.make_async_copy(back.at[me], out_ref.at[me], own_sem.at[2])
    home.start()
    exchange(back, out_ref, 16)
    home.wait()

    wait_for(x_hbm.at[others], send_sem.at[0])
    wait_for(obs_hbm.at[others], send_sem.at[1])
    wait_for(head_pair, send_sem.at[2])
    wait_for(gram_pair, send_sem.at[3])
    wait_for(all_but_one(head_plane), send_sem.at[4])
    wait_for(all_but_one(gram_plane), send_sem.at[5])
    wait_for(all_but_one(head_z), send_sem.at[6])
    wait_for(all_but_one(gram_z), send_sem.at[7])
    wait_for(all_but_one(head_all), send_sem.at[8])
    wait_for(gram_all.at[pl.ds(0, PLANE - 1)], send_sem.at[9])
    wait_for(gram_all.at[core_part], send_sem.at[10])
    wait_for(cross_pair, send_sem.at[11])
    wait_for(all_but_one(cross_plane), send_sem.at[12])
    wait_for(all_but_one(cross_z), send_sem.at[13])
    wait_for(cross_all.at[pl.ds(0, PLANE - 1)], send_sem.at[14])
    wait_for(cross_all.at[core_part], send_sem.at[15])
    wait_for(back.at[others], send_sem.at[16])
    wait_for(out_ref.at[others], recv_sem.at[16])


def body(states, observed, precision, up, up_bias, down, down_bias):
    def by_block(array):
        return array.reshape(OWNED, PEERS, BLOCK).transpose(1, 0, 2)

    hbm = pl.BlockSpec(memory_space=pltpu.HBM)
    slabs = (PEERS, OWNED, BLOCK)
    square = (MEMBERS, BLOCK)
    out = pl.pallas_call(
        kernel,
        out_shape=jax.ShapeDtypeStruct(slabs, BF16),
        in_specs=[hbm] * 7,
        out_specs=pl.BlockSpec(memory_space=pl.ANY),
        scratch_shapes=[
            pltpu.VMEM(slabs, BF16),
            pltpu.VMEM(slabs, BF16),
            pltpu.VMEM((PEERS * BLOCK // TILE, TILE), F32),
            pltpu.VMEM((PEERS, BLOCK), F32),
            pltpu.VMEM(up.shape, BF16),
            pltpu.VMEM(up_bias.shape, F32),
            pltpu.VMEM(down.shape, BF16),
            pltpu.VMEM(down_bias.shape, F32),
            pltpu.VMEM(slabs, BF16),
            pltpu.VMEM(slabs, BF16),
            pltpu.VMEM(square, BF16),
            pltpu.VMEM(square, BF16),
            pltpu.VMEM(square, BF16),
            pltpu.VMEM(square, BF16),
            pltpu.VMEM(slabs, BF16),
            pltpu.VMEM((HEAD * TILE, TILE), F32),
            pltpu.VMEM((HEAD * TILE, TILE), F32),
            pltpu.VMEM((PLANE, HEAD_ROWS, TILE), F32),
            pltpu.VMEM((PLANE, HEAD_ROWS, TILE), F32),
            pltpu.VMEM((NZ, HEAD_ROWS, TILE), F32),
            pltpu.VMEM((PLANE, HEAD_ROWS, TILE), F32),
            pltpu.VMEM(((len(LOWER) - HEAD) * TILE, TILE), F32),
            pltpu.VMEM((GRAM_ROWS * PLANE, TILE), F32),
            pltpu.VMEM((PLANE, GRAM_ROWS, TILE), F32),
            pltpu.VMEM((PLANE, GRAM_ROWS, TILE), F32),
            pltpu.VMEM((NZ, GRAM_ROWS, TILE), F32),
            pltpu.VMEM((CORES * PLANE, GRAM_ROWS, TILE), F32),
            pltpu.VMEM((CORES, MEMBERS // CORES, MEMBERS), F32),
            pltpu.VMEM((MEMBERS // CORES, MEMBERS), F32),
            pltpu.VMEM((PLANE, CROSS_ROWS, MEMBERS), F32),
            pltpu.VMEM((PLANE, CROSS_ROWS, MEMBERS), F32),
            pltpu.VMEM((NZ, CROSS_ROWS, MEMBERS), F32),
            pltpu.VMEM((CORES * PLANE, CROSS_ROWS, MEMBERS), F32),
            pltpu.VMEM((MEMBERS, MEMBERS), F32),
            pltpu.SemaphoreType.DMA((7,)),
            pltpu.SemaphoreType.DMA((3,)),
            pltpu.SemaphoreType.DMA((17,)),
            pltpu.SemaphoreType.DMA((17,)),
            pltpu.SemaphoreType.REGULAR,
        ],
        compiler_params=pltpu.CompilerParams(
            collective_id=0, has_side_effects=True, vmem_limit_bytes=56 << 20
        ),
        name="ensemble_update",
    )(
        by_block(states),
        by_block(observed),
        precision.reshape(PEERS * BLOCK // TILE, TILE),
        up,
        up_bias,
        down,
        down_bias,
    )
    return out.transpose(1, 0, 2).reshape(OWNED, PEERS * BLOCK)


def solution(mesh):
    return jax.shard_map(
        body,
        mesh=mesh,
        in_specs=(P("mem", "rep"), P("mem", "rep"), P("rep"), P(), P(), P(), P()),
        out_specs=P("mem", "rep"),
        check_vma=False,
    )
```

```python
import functools

import jax
import jax.numpy as jnp
from jax import lax
from jax.experimental import pallas as pl
from jax.experimental.pallas import tpu as pltpu
from jax.sharding import PartitionSpec as P

F32 = jnp.float32
BF16 = jnp.bfloat16
MESH = pl.DeviceIdType.MESH
PW = 256
LAYERS = 2
TILE = 128
NZ, NY, NX = 8, 4, 4
PLANE = NY * NX
PEERS = NZ * PLANE
CORES = 2
MEMBERS = 512
STATE = 131072
OWNED = MEMBERS // PEERS
BLOCK = STATE // CORES // PEERS
TILES = MEMBERS // TILE
LOWER = [(i, j) for i in range(TILES) for j in range(i + 1)]
HEAD = 2
HEAD_ROWS = HEAD * TILE // PLANE
GRAM_ROWS = (len(LOWER) - HEAD) * TILE // CORES // PLANE
PANEL = 16
CROSS_ROWS = MEMBERS // CORES // PLANE
CHUNK = 256
GROUPS = CHUNK // OWNED


def exact_dot(left, right):
    return jnp.dot(left, right, precision=lax.Precision.HIGHEST, preferred_element_type=F32)


def contract(left, right):
    return lax.dot_general(left, right, (((1,), (1,)), ((), ())), preferred_element_type=F32)


def repeated(tile, k):
    return jnp.broadcast_to(tile[k : k + 1, :], tile.shape)


def eliminate(a, first):
    tiles = range(PANEL // 8)
    last = first + PANEL
    sub = lax.broadcasted_iota(jnp.int32, (8, TILE), 0)
    lane = lax.broadcasted_iota(jnp.int32, (8, TILE), 1)
    rows = [a[first + 8 * t : first + 8 * t + 8, :] for t in tiles]
    own = (lane >= first) & (lane < last)
    fresh = [jnp.where(own, jnp.where(lane - first == sub + 8 * t, 1.0, 0.0), rows[t]) for t in tiles]
    cols = [
        [jnp.broadcast_to(rows[t][:, first + j : first + j + 1], (8, TILE)) for t in tiles]
        for j in range(PANEL)
    ]
    for k in range(PANEL):
        at, of = divmod(k, 8)
        pivot = cols[k]
        inverse = 1.0 / repeated(pivot[at], of)

        def reduced(column):
            row = repeated(column[at], of) * inverse
            out = [column[t] - pivot[t] * row for t in tiles]
            out[at] = jnp.where(sub == of, row, out[at])
            return out

        for j in range(k + 1, PANEL):
            cols[j] = reduced(cols[j])
        fresh = reduced(fresh)
    block = jnp.concatenate(fresh, axis=0)
    lanes = lax.broadcasted_iota(jnp.int32, (TILE, TILE), 1)
    rest = jnp.where((lanes >= first) & (lanes < last), 0.0, a)
    left = a[:, first:last]
    parts = []
    if first:
        parts.append(rest[:first] - exact_dot(left[:first], block))
    parts.append(block)
    if last < TILE:
        sums = [None] * 4
        for j in range(PANEL):
            term = jnp.broadcast_to(left[last : last + PANEL, j : j + 1], (PANEL, TILE)) * (
                jnp.broadcast_to(block[j : j + 1, :], (PANEL, TILE))
            )
            sums[j % 4] = term if sums[j % 4] is None else sums[j % 4] + term
        parts.append(rest[last : last + PANEL] - ((sums[0] + sums[1]) + (sums[2] + sums[3])))
    if last + PANEL < TILE:
        parts.append(rest[last + PANEL :] - exact_dot(left[last + PANEL :], block))
    return jnp.concatenate(parts, axis=0)


def eliminated(a, begin, end):
    for first in range(begin, end, PANEL):
        a = eliminate(a, first)
    return a


def tile_at(b):
    return slice(b * TILE, (b + 1) * TILE)


def advance(k_ref, b, inverse):
    own, following = tile_at(b), tile_at(b + 1)
    pivot = k_ref[following, following] - exact_dot(
        k_ref[following, own], exact_dot(inverse, k_ref[own, following])
    )
    rows = exact_dot(inverse, k_ref[own, :])
    cols = k_ref[:, own]
    scaled = exact_dot(cols, inverse)
    for i in range(TILES):
        for j in range(TILES):
            at = tile_at(i), tile_at(j)
            if i == b:
                k_ref[at] = inverse if j == b else rows[:, at[1]]
            elif j == b:
                k_ref[at] = -scaled[at[0], :]
            else:
                k_ref[at] = k_ref[at] - exact_dot(cols[at[0], :], rows[:, at[1]])
    return pivot


def forecast(x, up_ref, up_bias_ref, down_ref, down_bias_ref):
    for layer in range(LAYERS):
        half = 0.5 * (
            jnp.dot(x, up_ref[layer], preferred_element_type=F32) + up_bias_ref[layer : layer + 1, :]
        )
        hidden = (half + half * jnp.tanh(half)).astype(BF16)
        x = (
            x.astype(F32)
            + jnp.dot(hidden, down_ref[layer], preferred_element_type=F32)
            + down_bias_ref[layer : layer + 1, :]
        ).astype(BF16)
    return x


def wait_for(ref, sem):
    pltpu.make_async_copy(ref, ref, sem).wait()


def kernel(
    x_hbm, obs_hbm, prec_hbm, up_hbm, up_bias_hbm, down_hbm, down_bias_hbm, out_ref,
    x_own, obs_own, prec_in, prec, up, up_bias, down, down_bias, x_in, obs_in, pred, states, dev, weighted, back,
    head, head_pair, head_half, head_plane, head_z, head_all,
    gram, gram_pair, gram_half, gram_plane, gram_z, gram_all,
    cross, cross_pair, cross_half, cross_plane, cross_z, cross_all, kmat,
    load_sem, own_sem, send_sem, recv_sem, plane_in,
):
    me, core = lax.axis_index("mem"), lax.axis_index("rep")
    z, q = me // PLANE, lax.rem(me, PLANE)
    y, x = q // NX, lax.rem(q, NX)

    loads = [
        pltpu.make_async_copy(src, dst, load_sem.at[i])
        for i, (src, dst) in enumerate(
            [
                (up_hbm, up), (down_hbm, down), (up_bias_hbm, up_bias), (down_bias_hbm, down_bias),
                (prec_hbm, prec_in), (x_hbm, x_own), (obs_hbm, obs_own),
            ]
        )
    ]
    own_copies = [
        pltpu.make_async_copy(x_hbm.at[me], x_in.at[me], own_sem.at[0]),
        pltpu.make_async_copy(obs_hbm.at[me], obs_in.at[me], own_sem.at[1]),
    ]

    columns = [lax.rem(x + d, NX) for d in range(NX)]
    rows_of = [lax.rem(y + d, NY) * NX for d in range(NY)]
    layers = [lax.rem(z + d, NZ) * PLANE for d in range(NZ)]
    far_first = [4, 5, 3, 6, 2, 7, 1, 0]
    plane_peers = [rows_of[b] + columns[a] for b in (2, 1, 3, 0) for a in (2, 1, 3, 0)][:-1]
    column_peers = [layers[d] + q for d in far_first[:-1]]

    def for_peers(visit):
        def one(s, carry):
            side = lax.rem(y + s // NX + 1, NY) * NX + lax.rem(x + lax.rem(s, NX) + 1, NX)
            for d in far_first:
                visit(layers[d] + side)
            return carry

        lax.fori_loop(0, PLANE - 1, one, 0)
        for target in column_peers:
            visit(target)

    barrier = pltpu.get_barrier_semaphore()

    def greet(sem, targets):
        for target in targets:
            pl.semaphore_signal(sem, 1, device_id={"mem": target}, device_id_type=MESH)

    near = [z * PLANE + target for target in plane_peers]
    greet(barrier, near + column_peers)
    pl.semaphore_signal(barrier, 1, device_id={"rep": 1 - core}, device_id_type=MESH)
    for copy in own_copies + loads:
        copy.start()
    pl.semaphore_wait(barrier, PLANE + NZ - 1)
    greet(plane_in, column_peers)
    pl.semaphore_wait(plane_in, NZ - 1)

    def send(src, dst, i, target):
        pltpu.make_async_remote_copy(
            src_ref=src, dst_ref=dst, send_sem=send_sem.at[i], recv_sem=recv_sem.at[i],
            device_id=target, device_id_type=MESH,
        ).start()

    def exchange(src, dst, i):
        for_peers(lambda target: send(src.at[target], dst.at[me], i, {"mem": target}))

    def to_plane(src_of, dst, i):
        for target in plane_peers:
            send(src_of(target), dst, i, {"mem": z * PLANE + target})

    def to_column(src, dst, i):
        for target in column_peers:
            send(src, dst, i, {"mem": target})

    def to_core(src, dst, i):
        send(src, dst, i, {"rep": 1 - core})

    def summed(ref):
        total = ref[0]
        for n in range(1, ref.shape[0]):
            total = total + ref[n]
        return total

    def all_but_one(ref):
        return ref.at[pl.ds(0, ref.shape[0] - 1)]

    others = pl.ds(0, PEERS - 1)
    exchange(x_hbm, x_in, 0)
    exchange(obs_hbm, obs_in, 1)

    for copy in loads:
        copy.wait()
    for c in range(BLOCK // TILE):
        prec[:, c * TILE : (c + 1) * TILE] = prec_in[pl.ds(c, PEERS, stride=BLOCK // TILE), :]

    def misfit_of(c, total):
        at = pl.ds(pl.multiple_of(c * GROUPS, GROUPS), GROUPS)
        rows = x_own[at].reshape(CHUNK, BLOCK)
        seen = obs_own[at].reshape(CHUNK, BLOCK)
        for p in range(0, BLOCK, PW):
            said = forecast(rows[:, p : p + PW], up, up_bias, down, down_bias)
            resid = (seen[:, p : p + PW].astype(F32) - said.astype(F32)).astype(BF16).astype(F32)
            square = (resid * resid).reshape(GROUPS, OWNED, PW).sum(axis=1)
            total = total + square * prec[at, p : p + PW]
        return total

    misfit = jnp.sum(
        lax.fori_loop(0, MEMBERS // CHUNK, misfit_of, jnp.zeros((GROUPS, PW), F32))
    ) / (MEMBERS * STATE)

    own_copies[0].wait()
    wait_for(x_in.at[others], recv_sem.at[0])

    def forecast_block(c, carry):
        rows = x_in[pl.ds(pl.multiple_of(c * GROUPS, GROUPS), GROUPS)].reshape(CHUNK, BLOCK)
        at = pl.ds(pl.multiple_of(c * CHUNK, CHUNK), CHUNK)
        states[at, :] = rows
        for p in range(0, BLOCK, PW):
            pred[at, p : p + PW] = forecast(rows[:, p : p + PW], up, up_bias, down, down_bias)
        return carry

    lax.fori_loop(0, MEMBERS // CHUNK, forecast_block, 0)
    prec_row = prec[pl.ds(me, 1), :]
    wide = pred[...].astype(F32)
    dev[...] = (wide - jnp.mean(wide, axis=0, keepdims=True)).astype(BF16)
    weighted[...] = (dev[...].astype(F32) * prec_row).astype(BF16)
    eye = lax.broadcasted_iota(jnp.int32, (TILE, TILE), 0) == lax.broadcasted_iota(
        jnp.int32, (TILE, TILE), 1
    )
    def lower_block(i, j):
        part = contract(weighted[tile_at(i), :], dev[tile_at(j), :]) / STATE
        return part + jnp.where(eye, misfit, 0.0) if i == j else part

    for n, (i, j) in enumerate(LOWER[:HEAD]):
        head[tile_at(n), :] = lower_block(i, j)
    to_core(head, head_pair, 2)
    for n, (i, j) in enumerate(LOWER[HEAD:]):
        gram[tile_at(n), :] = lower_block(i, j)
    half = GRAM_ROWS * PLANE
    theirs = pl.ds(pl.multiple_of((1 - core) * half, 8), half)
    mine = pl.ds(pl.multiple_of(core * half, 8), half)
    to_core(gram.at[theirs], gram_pair, 3)
    wait_for(head_pair, recv_sem.at[2])
    head_half[...] = (head[...] + head_pair[...]).reshape(PLANE, HEAD_ROWS, TILE)
    to_plane(lambda target: head_half.at[target], head_plane.at[q], 4)
    wait_for(gram_pair, recv_sem.at[3])
    gram_half[...] = (gram[mine, :] + gram_pair[...]).reshape(PLANE, GRAM_ROWS, TILE)
    to_plane(lambda target: gram_half.at[target], gram_plane.at[q], 5)

    own_copies[1].wait()
    wait_for(obs_in.at[others], recv_sem.at[1])
    for c in range(MEMBERS // CHUNK):
        at = slice(c * CHUNK, (c + 1) * CHUNK)
        seen = obs_in[c * GROUPS : (c + 1) * GROUPS].reshape(CHUNK, BLOCK)
        resid = (seen.astype(F32) - pred[at, :].astype(F32)).astype(BF16)
        cross[c] = contract(resid, weighted[...]) / STATE
    to_core(cross.at[1 - core], cross_pair, 11)

    wide = states[...].astype(F32)
    dev[...] = (wide - jnp.mean(wide, axis=0, keepdims=True)).astype(BF16)
    wait_for(cross_pair, recv_sem.at[11])
    cross_half[...] = (cross[core] + cross_pair[...]).reshape(PLANE, CROSS_ROWS, MEMBERS)
    to_plane(lambda target: cross_half.at[target], cross_plane.at[q], 12)
    wait_for(all_but_one(head_plane), recv_sem.at[4])
    head_plane[q] = head_half[q]
    head_z[z] = summed(head_plane)
    to_column(head_z.at[z], head_z.at[z], 6)
    wait_for(all_but_one(gram_plane), recv_sem.at[5])
    gram_plane[q] = gram_half[q]
    gram_z[z] = summed(gram_plane)
    to_column(gram_z.at[z], gram_z.at[z], 7)
    wait_for(all_but_one(head_z), recv_sem.at[6])
    head_all[q] = summed(head_z)
    to_plane(lambda target: head_all.at[q], head_all.at[q], 8)
    wait_for(all_but_one(gram_z), recv_sem.at[7])
    own_part = core * PLANE + q
    gram_all[own_part] = summed(gram_z)
    to_plane(lambda target: gram_all.at[own_part], gram_all.at[own_part], 9)
    wait_for(all_but_one(cross_plane), recv_sem.at[12])
    cross_plane[q] = cross_half[q]
    cross_z[z] = summed(cross_plane)
    to_column(cross_z.at[z], cross_z.at[z], 13)

    below = lax.broadcasted_iota(jnp.int32, (TILE, TILE), 0) >= lax.broadcasted_iota(
        jnp.int32, (TILE, TILE), 1
    )

    def place(lower, blocks):
        for n, (i, j) in enumerate(blocks):
            part = lower[tile_at(n), :]
            if i == j:
                part = jnp.where(below, part, part.T) + jnp.where(eye, 1e-06, 0.0)
            else:
                kmat[tile_at(j), tile_at(i)] = part.T
            kmat[tile_at(i), tile_at(j)] = part

    wait_for(all_but_one(head_all), recv_sem.at[8])
    place(head_all[...].reshape(HEAD * TILE, TILE), LOWER[:HEAD])
    inverse = eliminated(kmat[tile_at(0), tile_at(0)], 0, TILE // 2)
    core_part = pl.ds(pl.multiple_of(core * PLANE, PLANE), PLANE)
    wait_for(gram_all.at[pl.ds(0, PLANE - 1)], recv_sem.at[9])
    to_core(gram_all.at[core_part], gram_all.at[core_part], 10)
    inverse = eliminated(inverse, TILE // 2, TILE)
    wait_for(all_but_one(cross_z), recv_sem.at[13])
    cross_all[own_part] = summed(cross_z)
    to_plane(lambda target: cross_all.at[own_part], cross_all.at[own_part], 14)
    wait_for(gram_all.at[core_part], recv_sem.at[10])
    place(gram_all[...].reshape((len(LOWER) - HEAD) * TILE, TILE), LOWER[HEAD:])
    inverse = eliminated(advance(kmat, 0, inverse), 0, TILE)
    inverse = eliminated(advance(kmat, 1, inverse), 0, TILE)
    wait_for(cross_all.at[pl.ds(0, PLANE - 1)], recv_sem.at[14])
    to_core(cross_all.at[core_part], cross_all.at[core_part], 15)
    inverse = eliminated(advance(kmat, 2, inverse), 0, TILE // 2)
    wait_for(cross_all.at[core_part], recv_sem.at[15])

    head_cols = slice(0, MEMBERS - TILE)
    tail_cols = slice(MEMBERS - TILE, MEMBERS)
    whole = cross_all[...].reshape(MEMBERS, MEMBERS)
    before = exact_dot(whole[:, head_cols], kmat[head_cols, head_cols])
    left = whole[:, tail_cols] - exact_dot(whole[:, head_cols], kmat[head_cols, tail_cols])
    inverse = eliminated(inverse, TILE // 2, TILE)
    last = exact_dot(left, inverse)
    mixing = jnp.concatenate(
        [before + exact_dot(last, kmat[tail_cols, head_cols]), last], axis=1
    ).astype(BF16)
    for c in range(MEMBERS // CHUNK):
        at = slice(c * CHUNK, (c + 1) * CHUNK)
        moved = jnp.dot(mixing[at, :], dev[...], preferred_element_type=F32)
        fresh = (states[at, :].astype(F32) + moved).astype(BF16)
        back[c * GROUPS : (c + 1) * GROUPS] = fresh.reshape(GROUPS, OWNED, BLOCK)
    home = pltpu.make_async_copy(back.at[me], out_ref.at[me], own_sem.at[2])
    home.start()
    exchange(back, out_ref, 16)
    home.wait()

    wait_for(x_hbm.at[others], send_sem.at[0])
    wait_for(obs_hbm.at[others], send_sem.at[1])
    wait_for(head_pair, send_sem.at[2])
    wait_for(gram_pair, send_sem.at[3])
    wait_for(all_but_one(head_plane), send_sem.at[4])
    wait_for(all_but_one(gram_plane), send_sem.at[5])
    wait_for(all_but_one(head_z), send_sem.at[6])
    wait_for(all_but_one(gram_z), send_sem.at[7])
    wait_for(all_but_one(head_all), send_sem.at[8])
    wait_for(gram_all.at[pl.ds(0, PLANE - 1)], send_sem.at[9])
    wait_for(gram_all.at[core_part], send_sem.at[10])
    wait_for(cross_pair, send_sem.at[11])
    wait_for(all_but_one(cross_plane), send_sem.at[12])
    wait_for(all_but_one(cross_z), send_sem.at[13])
    wait_for(cross_all.at[pl.ds(0, PLANE - 1)], send_sem.at[14])
    wait_for(cross_all.at[core_part], send_sem.at[15])
    wait_for(back.at[others], send_sem.at[16])
    wait_for(out_ref.at[others], recv_sem.at[16])


def body(states, observed, precision, up, up_bias, down, down_bias):
    def by_block(array):
        return array.reshape(OWNED, PEERS, BLOCK).transpose(1, 0, 2)

    hbm = pl.BlockSpec(memory_space=pltpu.HBM)
    slabs = (PEERS, OWNED, BLOCK)
    square = (MEMBERS, BLOCK)
    out = pl.pallas_call(
        kernel,
        out_shape=jax.ShapeDtypeStruct(slabs, BF16),
        in_specs=[hbm] * 7,
        out_specs=pl.BlockSpec(memory_space=pl.ANY),
        scratch_shapes=[
            pltpu.VMEM(slabs, BF16),
            pltpu.VMEM(slabs, BF16),
            pltpu.VMEM((PEERS * BLOCK // TILE, TILE), F32),
            pltpu.VMEM((PEERS, BLOCK), F32),
            pltpu.VMEM(up.shape, BF16),
            pltpu.VMEM(up_bias.shape, F32),
            pltpu.VMEM(down.shape, BF16),
            pltpu.VMEM(down_bias.shape, F32),
            pltpu.VMEM(slabs, BF16),
            pltpu.VMEM(slabs, BF16),
            pltpu.VMEM(square, BF16),
            pltpu.VMEM(square, BF16),
            pltpu.VMEM(square, BF16),
            pltpu.VMEM(square, BF16),
            pltpu.VMEM(slabs, BF16),
            pltpu.VMEM((HEAD * TILE, TILE), F32),
            pltpu.VMEM((HEAD * TILE, TILE), F32),
            pltpu.VMEM((PLANE, HEAD_ROWS, TILE), F32),
            pltpu.VMEM((PLANE, HEAD_ROWS, TILE), F32),
            pltpu.VMEM((NZ, HEAD_ROWS, TILE), F32),
            pltpu.VMEM((PLANE, HEAD_ROWS, TILE), F32),
            pltpu.VMEM(((len(LOWER) - HEAD) * TILE, TILE), F32),
            pltpu.VMEM((GRAM_ROWS * PLANE, TILE), F32),
            pltpu.VMEM((PLANE, GRAM_ROWS, TILE), F32),
            pltpu.VMEM((PLANE, GRAM_ROWS, TILE), F32),
            pltpu.VMEM((NZ, GRAM_ROWS, TILE), F32),
            pltpu.VMEM((CORES * PLANE, GRAM_ROWS, TILE), F32),
            pltpu.VMEM((CORES, MEMBERS // CORES, MEMBERS), F32),
            pltpu.VMEM((MEMBERS // CORES, MEMBERS), F32),
            pltpu.VMEM((PLANE, CROSS_ROWS, MEMBERS), F32),
            pltpu.VMEM((PLANE, CROSS_ROWS, MEMBERS), F32),
            pltpu.VMEM((NZ, CROSS_ROWS, MEMBERS), F32),
            pltpu.VMEM((CORES * PLANE, CROSS_ROWS, MEMBERS), F32),
            pltpu.VMEM((MEMBERS, MEMBERS), F32),
            pltpu.SemaphoreType.DMA((7,)),
            pltpu.SemaphoreType.DMA((3,)),
            pltpu.SemaphoreType.DMA((17,)),
            pltpu.SemaphoreType.DMA((17,)),
            pltpu.SemaphoreType.REGULAR,
        ],
        compiler_params=pltpu.CompilerParams(
            collective_id=0, has_side_effects=True, vmem_limit_bytes=56 << 20
        ),
        name="ensemble_update",
    )(
        by_block(states),
        by_block(observed),
        precision.reshape(PEERS * BLOCK // TILE, TILE),
        up,
        up_bias,
        down,
        down_bias,
    )
    return out.transpose(1, 0, 2).reshape(OWNED, PEERS * BLOCK)


def solution(mesh):
    return jax.shard_map(
        body,
        mesh=mesh,
        in_specs=(P("mem", "rep"), P("mem", "rep"), P("rep"), P(), P(), P(), P()),
        out_specs=P("mem", "rep"),
        check_vma=False,
    )
```
